32 devices in a mesh: aux: 8 (over z, x), occ: 4 (over y, core).
Axes of the slice: x: 2, y: 2, z: 4, core: 2. Of those that a mesh axis runs over, the one named last changes fastest.
Arguments:
- factors: bfloat16 [3840, 8, 2560], P('aux', 'occ'), may hold values from -0.25 to 0.25
- pair_list: int32 [4, 2], replicated, may hold values from 0 to 3
- eps_occ: float32 [8], replicated, may hold values from -2 to -0.3
- eps_virt: float32 [2560], replicated, may hold values from 0.2 to 3
Outputs:
- energy_by_virtual: float32 [4, 4, 2560], P('occ', None, 'aux')
The draws below stay inside these ranges and needn't reach their ends.
All inputs are finite; a program needn't handle non-finite values.
Results may differ from the reference program's by a relative error of at most 0.0003.
Values may be sent and summed in bfloat16 or wider, within the bound.
A program may use at most 192 MiB of HBM per device.

```python
import jax
import jax.numpy as jnp
from jax import lax

NAUX = 3840
W = 2560
ORB_DEV = 2
NORB = 8
NPAIR = 4
N_OCC = 4


def plant(entries, rng, least, largest):
    dims = entries.shape
    index_at = [jax.random.randint(jax.random.fold_in(rng, axis), (), 0, dims[axis]) for axis in range(len(dims))]
    entries = entries.at[tuple(index_at)].set(least)
    longest = dims.index(max(dims))
    index_at[longest] = (index_at[longest] + 1) % dims[longest]
    return entries.at[tuple(index_at)].set(largest)


def block_levels(own_key, shape, shards, low, high):
    factor_of = 1.0
    for position, blocks in shards:
        draws = jax.random.uniform(jax.random.fold_in(jax.random.fold_in(own_key, 6), position), (blocks,), jnp.float32, low / len(shards), high / len(shards))
        factor_of = factor_of * jnp.repeat(jnp.exp(draws), shape[position] // blocks).reshape((-1,) + (1,) * (len(shape) - 1 - position))
    return factor_of


def gaussian(stream_key, dims, scale, most, shards=(), kind=jnp.bfloat16):
    gain = block_levels(stream_key, dims, shards, -0.22, 0.18) if shards else 1.0
    values = jax.random.normal(stream_key, dims, jnp.float32) * scale * gain
    return jnp.minimum(jnp.maximum(values, -most), most).astype(kind)


def setup_inputs(seed: int = 0) -> dict:
    seeds = jax.random.split(jax.random.key(seed), 5)
    return {
        "factors": gaussian(seeds[0], (NAUX, NORB, W), ((W * NAUX) ** -0.25), 0.25, ((0, 8), (1, 4))),
        "pair_list": plant(jax.random.randint(seeds[1], (NPAIR, 2), 0, N_OCC), jax.random.fold_in(seeds[1], 1), 0, N_OCC - 1).astype(jnp.int32),
        "eps_occ": jnp.clip(jax.random.uniform(seeds[2], (NORB,), jnp.float32, -2.0, -0.3), -2.0, -0.3),
        "eps_virt": jnp.clip(jax.random.uniform(seeds[3], (W,), jnp.float32, 0.2, 3.0), 0.2, 3.0),
    }


def reference(factors, pair_list, eps_occ, eps_virt):
    def block_energy(pair_row):
        def orbital_pair(flat):
            left_index = (pair_row[0] * ORB_DEV + flat // ORB_DEV).astype(jnp.int32)
            right_index = (pair_row[1] * ORB_DEV + flat % ORB_DEV).astype(jnp.int32)
            left_orb = lax.dynamic_index_in_dim(factors, left_index, 1, keepdims=False)
            right_orb = lax.dynamic_index_in_dim(factors, right_index, 1, keepdims=False)
            coulomb = jnp.dot(left_orb.T, right_orb, preferred_element_type=jnp.float32)
            denominator = eps_virt[:, None] + eps_virt[None, :] - eps_occ[left_index] - eps_occ[right_index]
            return -jnp.sum(coulomb * (2.0 * coulomb - coulomb.T) / denominator, axis=1)

        return lax.map(orbital_pair, jnp.arange(ORB_DEV * ORB_DEV, dtype=jnp.int32))

    return lax.map(block_energy, pair_list)
```

```python
import functools

import jax
import jax.numpy as jnp
from jax import lax
from jax.experimental import pallas as pl
from jax.experimental.pallas import tpu as pltpu
from jax.sharding import PartitionSpec as P

MESH = pl.DeviceIdType.MESH


def flip(z, k):
    return (z // 2 + k // 2) % 2 * 2 + (z + k) % 2


def route(planes, slices, sel, gath, zbuf, z_send, z_recv, hop_send, hop_recv, core_send, core_recv):
    depth, width = sel.shape[3], sel.shape[4]
    rows = depth // slices
    steps = planes * slices
    aux = lax.axis_index("aux")
    occ = lax.axis_index("occ")
    z, x, y, c = aux // 2, aux % 2, occ // 2, occ % 2

    def device(z_, x_, y_, c_):
        return {"aux": z_ * 2 + x_, "occ": y_ * 2 + c_}

    partners = [device(flip(z, k), x, y, c) for k in range(1, planes)]
    partners += [device(z, 1 - x, y, c), device(z, x, 1 - y, c), device(z, x, y, 1 - c)]
    barrier = pltpu.get_barrier_semaphore()
    for partner in partners:
        pl.semaphore_signal(barrier, inc=1, device_id=partner, device_id_type=MESH)
    pl.semaphore_wait(barrier, len(partners))

    def span(t):
        return pl.ds(pl.multiple_of(t * rows, 16), rows)

    def place(s, zs, xs, ys, cs, t):
        first = pl.multiple_of((zs * 2 + xs) * depth + t * rows, 16)
        left = pl.multiple_of((ys * 2 + cs) * width, 128)
        return gath.at[s, pl.ds(first, rows), pl.ds(left, width)]

    def z_copy(t, k, s, rel):
        zt = flip(z, k)
        own = x if s == 0 else y
        w = own if rel == 0 else 1 - own
        dst = place(s, z, x, y, c, t) if rel == 0 else zbuf.at[k, s, span(t), :]
        return pltpu.make_async_remote_copy(
            src_ref=sel.at[zt, s, w, span(t), :],
            dst_ref=dst,
            send_sem=z_send.at[t, k, s, rel],
            recv_sem=z_recv.at[t, k, s, rel],
            device_id=device(zt, x, y, c),
            device_id_type=MESH,
        )

    def z_keep(t, s, rel):
        own = x if s == 0 else y
        w = own if rel == 0 else 1 - own
        dst = place(s, z, x, y, c, t) if rel == 0 else zbuf.at[0, s, span(t), :]
        return pltpu.make_async_copy(sel.at[z, s, w, span(t), :], dst, z_recv.at[t, 0, s, rel])

    def hop(n, s, kind):
        t, k = n // planes, n % planes
        zs = flip(z, k)
        share = device(z, x, 1 - y, c) if s == 0 else device(z, 1 - x, y, c)
        other = device(z, 1 - x, y, c) if s == 0 else device(z, x, 1 - y, c)
        xs, ys = (1 - x, y) if s == 0 else (x, 1 - y)
        mine = place(s, zs, x, y, c, t)
        if kind == 0:
            src, dst, target = mine, mine, share
        elif kind == 1:
            src, dst, target = zbuf.at[k, s, span(t), :], mine, other
        else:
            src = place(s, zs, xs, ys, c, t)
            dst, target = src, share
        return pltpu.make_async_remote_copy(
            src_ref=src,
            dst_ref=dst,
            send_sem=hop_send.at[n, s, kind],
            recv_sem=hop_recv.at[n, s, kind],
            device_id=target,
            device_id_type=MESH,
        )

    def across(n, s, kind):
        t, k = n // planes, n % planes
        zs = flip(z, k)
        if s == 0:
            spots = [(x, y), (x, 1 - y), (1 - x, y), (1 - x, 1 - y)]
        else:
            spots = [(x, y), (1 - x, y), (x, 1 - y), (1 - x, 1 - y)]
        ref = place(s, zs, spots[kind][0], spots[kind][1], c, t)
        return pltpu.make_async_remote_copy(
            src_ref=ref,
            dst_ref=ref,
            send_sem=core_send.at[n, s, kind],
            recv_sem=core_recv.at[n, s, kind],
            device_id=device(z, x, y, 1 - c),
            device_id_type=MESH,
        )

    @pl.loop(0, slices)
    def _(t):
        for s in range(2):
            for rel in (1, 0):
                z_keep(t, s, rel).start()
                for k in (2, 3, 1):
                    z_copy(t, k, s, rel).start()

    @pl.loop(0, steps + 2)
    def _(n):
        @pl.when(n < steps)
        def _():
            t, k = n // planes, n % planes
            for s in range(2):
                for rel in (1, 0):

                    @pl.when(k == 0)
                    def _():
                        z_keep(t, s, rel).wait()

                    @pl.when(k > 0)
                    def _():
                        z_copy(t, k, s, rel).wait_recv()

                    hop(n, s, rel).start()
                    if rel == 0:
                        across(n, s, 0).start()

        @pl.when((n >= 1) & (n < steps + 1))
        def _():
            for s in range(2):
                hop(n - 1, s, 1).wait_recv()
                hop(n - 1, s, 2).start()
                across(n - 1, s, 2).start()

        @pl.when(n >= 2)
        def _():
            for s in range(2):
                hop(n - 2, s, 0).wait_recv()
                across(n - 2, s, 1).start()
                hop(n - 2, s, 2).wait_recv()
                across(n - 2, s, 3).start()

    @pl.loop(0, slices)
    def _(t):
        for s in range(2):
            for rel in (1, 0):
                for k in (2, 3, 1):
                    z_copy(t, k, s, rel).wait_send()

    @pl.loop(0, steps)
    def _(n):
        for s in range(2):
            for kind in range(3):
                hop(n, s, kind).wait_send()
            for kind in range(4):
                across(n, s, kind).wait()


def by_planes(factors, pair_list, eps_occ, eps_virt):
    local_q, orb_local, virt = factors.shape
    n_aux = lax.axis_size("aux")
    n_occ = lax.axis_size("occ")
    planes = pair_list.shape[0]
    width = virt // n_occ
    slices = 3 if local_q % 48 == 0 else 1
    steps = planes * slices
    aux = lax.axis_index("aux")
    occ = lax.axis_index("occ")
    z, x, y, c = aux // 2, aux % 2, occ // 2, occ % 2

    mine = factors.transpose(1, 0, 2)
    quarter = lax.all_to_all(mine, "occ", split_axis=2, concat_axis=0, tiled=True)
    blocks = quarter.reshape(n_occ, orb_local, local_q, width)
    sel = jnp.concatenate(
        [lax.dynamic_slice_in_dim(blocks, pair_list[p, s], 1, 0) for p in range(planes) for s in range(2)], axis=0
    ).reshape(planes, 2, orb_local, local_q, width)

    gath, _ = pl.pallas_call(
        functools.partial(route, planes, slices),
        out_shape=[
            jax.ShapeDtypeStruct((2, n_aux * local_q, virt), factors.dtype),
            jax.ShapeDtypeStruct((planes, 2, local_q, width), factors.dtype),
        ],
        in_specs=[pl.BlockSpec(memory_space=pl.ANY)],
        out_specs=[pl.BlockSpec(memory_space=pl.ANY)] * 2,
        scratch_shapes=[
            pltpu.SemaphoreType.DMA((slices, planes, 2, 2)),
            pltpu.SemaphoreType.DMA((slices, planes, 2, 2)),
            pltpu.SemaphoreType.DMA((steps, 2, 3)),
            pltpu.SemaphoreType.DMA((steps, 2, 3)),
            pltpu.SemaphoreType.DMA((steps, 2, 4)),
            pltpu.SemaphoreType.DMA((steps, 2, 4)),
        ],
        compiler_params=pltpu.CompilerParams(collective_id=0, has_side_effects=True),
    )(sel)

    half = virt // 2
    chosen = lax.dynamic_index_in_dim(pair_list, z, 0, keepdims=False)
    e_i = lax.dynamic_index_in_dim(eps_occ, chosen[0] * orb_local + x, 0, keepdims=False)
    e_j = lax.dynamic_index_in_dim(eps_occ, chosen[1] * orb_local + y, 0, keepdims=False)
    contract = (((0,), (0,)), ((), ()))
    tiles = []
    for t in range(2):
        t_col = (t + c) % 2
        cols = lax.dynamic_slice_in_dim(gath[1], t_col * half, half, 1)
        tiles.append(
            lax.dot_general(gath[0, :, t * half : (t + 1) * half], cols, contract, preferred_element_type=jnp.float32)
        )
    sums = []
    for t in range(2):
        t_col = (t + c) % 2
        swapped = jnp.where(c == 0, tiles[t], tiles[1 - t]).T
        rows_e = eps_virt[t * half : (t + 1) * half]
        cols_e = lax.dynamic_slice_in_dim(eps_virt, t_col * half, half)
        denominator = rows_e[:, None] + cols_e[None, :] - e_i - e_j
        sums.append(-jnp.sum(tiles[t] * (2.0 * tiles[t] - swapped) / denominator, axis=1))
    part = jnp.concatenate(sums)

    spread = lax.all_to_all(part.reshape(n_aux, virt // n_aux), "aux", split_axis=0, concat_axis=0, tiled=True)
    every = lax.all_gather(spread, "occ", axis=0, tiled=False)
    every = every.reshape(2, 2, planes, 2, virt // n_aux).sum(axis=1)
    own = lax.dynamic_index_in_dim(every, occ, 1, keepdims=False)
    return own.transpose(1, 0, 2).reshape(1, 4, virt // n_aux)


def by_groups(factors, pair_list, eps_occ, eps_virt):
    local_q, orb_local, virt_width = factors.shape
    aux_count = lax.axis_size("aux")
    my_group = lax.axis_index("occ")
    chosen = pair_list[my_group]
    everyone = lax.all_gather(factors, "occ", axis=1, tiled=True)
    first_block = lax.dynamic_slice_in_dim(everyone, chosen[0] * orb_local, orb_local, 1)
    second = lax.dynamic_slice_in_dim(everyone, chosen[1] * orb_local, orb_local, 1)
    picked = jnp.stack([first_block, second], axis=0)
    rows_grid = 2 ** ((aux_count.bit_length() - 1) // 2)
    cols_grid = aux_count // rows_grid
    span_a = virt_width // rows_grid
    span_b = virt_width // cols_grid
    rows_pieces = picked.reshape(2, local_q, orb_local, rows_grid, span_a).transpose(3, 0, 1, 2, 4)
    rows_pieces = jnp.tile(rows_pieces, (cols_grid, 1, 1, 1, 1))
    cols_pieces = picked.reshape(2, local_q, orb_local, cols_grid, span_b).transpose(3, 0, 1, 2, 4)
    cols_pieces = jnp.repeat(cols_pieces, rows_grid, axis=0)
    send_pieces = jnp.concatenate([rows_pieces, cols_pieces], axis=4)
    regrouped = lax.all_to_all(send_pieces, "aux", split_axis=0, concat_axis=2, tiled=True)[0]
    aux_rank = lax.axis_index("aux")
    row_id = aux_rank % rows_grid
    col_id = aux_rank // rows_grid
    contract = (((0,), (0,)), ((), ()))
    direct = lax.dot_general(
        regrouped[0, :, :, :span_a], regrouped[1, :, :, span_a:], contract, preferred_element_type=jnp.float32
    )
    swapped = lax.dot_general(
        regrouped[1, :, :, :span_a], regrouped[0, :, :, span_a:], contract, preferred_element_type=jnp.float32
    )
    swapped = swapped.transpose(2, 1, 0, 3)
    virt_rows = lax.dynamic_slice_in_dim(eps_virt, row_id * span_a, span_a)
    virt_cols = lax.dynamic_slice_in_dim(eps_virt, col_id * span_b, span_b)
    occ_left = lax.dynamic_slice_in_dim(eps_occ, chosen[0] * orb_local, orb_local)
    occ_right = lax.dynamic_slice_in_dim(eps_occ, chosen[1] * orb_local, orb_local)
    denominator = (
        virt_rows[None, :, None, None]
        + virt_cols[None, None, None, :]
        - occ_left[:, None, None, None]
        - occ_right[None, None, :, None]
    )
    partial_value = -jnp.sum(direct * (2.0 * direct - swapped) / denominator, axis=3)
    partial_value = partial_value.transpose(0, 2, 1).reshape(orb_local * orb_local, span_a)
    spread = lax.dynamic_update_slice_in_dim(
        jnp.zeros((orb_local * orb_local, virt_width), jnp.float32), partial_value, row_id * span_a, 1
    )
    shares = lax.psum_scatter(spread, "aux", scatter_dimension=1, tiled=True)
    return shares.reshape(1, orb_local * orb_local, -1)


def solution(mesh):
    def on_device(factors, pair_list, eps_occ, eps_virt):
        planes = pair_list.shape[0]
        fits = (
            mesh.shape["aux"] == 2 * planes
            and mesh.shape["occ"] == 4
            and planes == 4
            and factors.shape[1] == 2
            and factors.shape[0] % 16 == 0
            and factors.shape[2] % 512 == 0
        )
        body = by_planes if fits else by_groups
        return body(factors, pair_list, eps_occ, eps_virt)

    return jax.shard_map(
        on_device,
        mesh=mesh,
        in_specs=(P("aux", "occ", None), P(), P(), P()),
        out_specs=P("occ", None, "aux"),
        check_vma=False,
    )
```

```python
import functools

import jax
import jax.numpy as jnp
from jax import lax
from jax.experimental import pallas as pl
from jax.experimental.pallas import tpu as pltpu
from jax.sharding import PartitionSpec as P

MESH = pl.DeviceIdType.MESH


def flip(z, k):
    return (z // 2 + k // 2) % 2 * 2 + (z + k) % 2


def route(
    planes, slices, pairs, near, far, mine, part, gath, zbuf, quarter, sel, acc, held, turned,
    o_send, o_recv, z_send, z_recv, hop_send, hop_recv, core_send, core_recv, held_sem,
):
    depth, virt = mine.shape[1], mine.shape[2]
    rows = depth // slices
    width = virt // 4
    half = virt // 2
    steps = planes * slices
    aux = lax.axis_index("aux")
    occ = lax.axis_index("occ")
    z, x, y, c = aux // 2, aux % 2, occ // 2, occ % 2

    def device(z_, x_, y_, c_):
        return {"aux": z_ * 2 + x_, "occ": y_ * 2 + c_}

    def fellow(d):
        return {"aux": aux, "occ": flip(occ, d)}

    partners = [device(flip(z, k), x, y, c) for k in range(1, planes)]
    partners += [fellow(d) for d in range(1, 4)] + [device(z, 1 - x, y, c)]
    barrier = pltpu.get_barrier_semaphore()
    for partner in partners:
        pl.semaphore_signal(barrier, inc=1, device_id=partner, device_id_type=MESH)
    pl.semaphore_wait(barrier, len(partners))

    def span(t):
        return pl.ds(pl.multiple_of(t * rows, 16), rows)

    def place(s, zs, xs, ys, cs, t):
        first = pl.multiple_of((zs * 2 + xs) * depth + t * rows, 16)
        left = pl.multiple_of((ys * 2 + cs) * width, 128)
        return gath.at[s, pl.ds(first, rows), pl.ds(left, width)]

    def o_copy(t, d):
        to = flip(occ, d)
        src = mine.at[:, pl.ds(t * rows, rows), pl.ds(pl.multiple_of(to * width, 128), width)]
        if d == 0:
            return pltpu.make_async_copy(src, quarter[t].at[occ], o_recv.at[t, 0])
        return pltpu.make_async_remote_copy(
            src_ref=src,
            dst_ref=quarter[t].at[occ],
            send_sem=o_send.at[t, d],
            recv_sem=o_recv.at[t, d],
            device_id=fellow(d),
            device_id_type=MESH,
        )

    def z_copy(t, k, s, rel):
        zt = flip(z, k)
        own = x if s == 0 else y
        w = own if rel == 0 else 1 - own
        dst = place(s, z, x, y, c, t) if rel == 0 else zbuf.at[k, s, span(t), :]
        return pltpu.make_async_remote_copy(
            src_ref=sel.at[t, zt, s, w],
            dst_ref=dst,
            send_sem=z_send.at[t, k, s, rel],
            recv_sem=z_recv.at[t, k, s, rel],
            device_id=device(zt, x, y, c),
            device_id_type=MESH,
        )

    def z_keep(t, s, rel):
        own = x if s == 0 else y
        w = own if rel == 0 else 1 - own
        dst = place(s, z, x, y, c, t) if rel == 0 else zbuf.at[0, s, span(t), :]
        return pltpu.make_async_copy(sel.at[t, z, s, w], dst, z_recv.at[t, 0, s, rel])

    def hop(n, s, kind):
        t, k = n // planes, n % planes
        zs = flip(z, k)
        share = device(z, x, 1 - y, c) if s == 0 else device(z, 1 - x, y, c)
        other = device(z, 1 - x, y, c) if s == 0 else device(z, x, 1 - y, c)
        xs, ys = (1 - x, y) if s == 0 else (x, 1 - y)
        own = place(s, zs, x, y, c, t)
        if kind == 0:
            src, dst, target = own, own, share
        elif kind == 1:
            src, dst, target = zbuf.at[k, s, span(t), :], own, other
        else:
            src = place(s, zs, xs, ys, c, t)
            dst, target = src, share
        return pltpu.make_async_remote_copy(
            src_ref=src,
            dst_ref=dst,
            send_sem=hop_send.at[n, s, kind],
            recv_sem=hop_recv.at[n, s, kind],
            device_id=target,
            device_id_type=MESH,
        )

    def across(n, s, kind):
        t, k = n // planes, n % planes
        zs = flip(z, k)
        if s == 0:
            spots = [(x, y), (x, 1 - y), (1 - x, y), (1 - x, 1 - y)]
        else:
            spots = [(x, y), (1 - x, y), (x, 1 - y), (1 - x, 1 - y)]
        ref = place(s, zs, spots[kind][0], spots[kind][1], c, t)
        return pltpu.make_async_remote_copy(
            src_ref=ref,
            dst_ref=ref,
            send_sem=core_send.at[n, s, kind],
            recv_sem=core_recv.at[n, s, kind],
            device_id=device(z, x, y, 1 - c),
            device_id_type=MESH,
        )

    def fetch(t, s, q):
        first = pl.multiple_of(q * depth + t * rows, 16)
        return pltpu.make_async_copy(
            gath.at[s, pl.ds(first, rows), :],
            held.at[t % 2, s, pl.ds(q * rows, rows), :],
            held_sem.at[t % 2, s, q],
        )

    def start_exchange(t):
        for d in (2, 3, 1, 0):
            o_copy(t, d).start()

    def choose(t):
        for d in (0, 1, 2, 3):
            if d == 0:
                o_copy(t, d).wait()
            else:
                o_copy(t, d).wait_recv()
        if t + 2 < slices:
            start_exchange(t + 2)
        for p in range(planes):
            for s in range(2):
                block = pairs[p, s]
                for w in range(2):
                    sel[t, p, s, w] = quarter[t][block, w]
        for s in range(2):
            for rel in (1, 0):
                z_keep(t, s, rel).start()
                for k in (2, 3, 1):
                    z_copy(t, k, s, rel).start()

    start_exchange(0)
    if slices > 1:
        start_exchange(1)

    @pl.loop(0, 2 * (half // 128))
    def _(r):
        tile, blk = r // (half // 128), r % (half // 128)
        acc[tile, pl.ds(pl.multiple_of(blk * 128, 128), 128), :] = jnp.zeros((128, half), jnp.float32)

    choose(0)

    @pl.loop(0, steps + 8)
    def _(n):
        for t in range(1, slices):

            @pl.when(n == max(0, planes * t - 6))
            def _():
                choose(t)

        @pl.when(n < steps)
        def _():
            t, k = n // planes, n % planes
            for s in range(2):
                for rel in (1, 0):

                    @pl.when(k == 0)
                    def _():
                        z_keep(t, s, rel).wait()

                    @pl.when(k > 0)
                    def _():
                        z_copy(t, k, s, rel).wait_recv()

                    hop(n, s, rel).start()
                    if rel == 0:
                        across(n, s, 0).start()

        @pl.when((n >= 1) & (n < steps + 1))
        def _():
            for s in range(2):
                hop(n - 1, s, 1).wait_recv()
                hop(n - 1, s, 2).start()
                across(n - 1, s, 2).start()

        @pl.when((n >= 2) & (n < steps + 2))
        def _():
            for s in range(2):
                hop(n - 2, s, 0).wait_recv()
                across(n - 2, s, 1).start()
                hop(n - 2, s, 2).wait_recv()
                across(n - 2, s, 3).start()

        @pl.when((n >= 3) & (n < steps + 3))
        def _():
            for s in range(2):
                for kind in range(4):
                    across(n - 3, s, kind).wait_recv()

        @pl.when((n >= 6) & (n < steps + 6) & (n % planes == 2))
        def _():
            t = (n - 6) // planes
            for s in range(2):
                for q in range(2 * planes):
                    fetch(t, s, q).start()

        @pl.when(n >= 8)
        def _():
            t, unit = (n - 8) // planes, n % planes

            @pl.when(unit == 0)
            def _():
                for s in range(2):
                    for q in range(2 * planes):
                        fetch(t, s, q).wait()

            tile = unit // 2
            top = pl.multiple_of(unit % 2 * width, 128)
            left = pl.multiple_of((tile + c) % 2 * half, 128)
            lhs = pl.multiple_of(tile * half + unit % 2 * width, 128)
            turned[...] = held[t % 2, 0, :, pl.ds(lhs, width)].T

            @pl.loop(0, half // 256)
            def _(col):
                cols = pl.ds(pl.multiple_of(left + col * 256, 128), 256)
                into = pl.ds(pl.multiple_of(col * 256, 128), 256)
                acc[tile, pl.ds(top, width), into] += jnp.dot(
                    turned[...], held[t % 2, 1, :, cols], preferred_element_type=jnp.float32
                )

    @pl.loop(0, 2 * (half // 128))
    def _(r):
        tile, blk = r // (half // 128), r % (half // 128)
        at = pl.ds(pl.multiple_of(blk * 128, 128), 128)
        direct = acc[tile, at, :].T
        swapped = acc[(tile + c) % 2, :, at]
        denominator = far[tile] + near[tile, :, at]
        value = direct * (2.0 * direct - swapped) / denominator
        part[tile, :, at] = -jnp.sum(value, axis=0, keepdims=True)

    for t in range(slices):
        for d in (1, 2, 3):
            o_copy(t, d).wait_send()

    @pl.loop(0, slices)
    def _(t):
        for s in range(2):
            for rel in (1, 0):
                for k in (2, 3, 1):
                    z_copy(t, k, s, rel).wait_send()

    @pl.loop(0, steps)
    def _(n):
        for s in range(2):
            for kind in range(3):
                hop(n, s, kind).wait_send()
            for kind in range(4):
                across(n, s, kind).wait_send()


def by_planes(factors, pair_list, eps_occ, eps_virt):
    local_q, orb_local, virt = factors.shape
    n_aux = lax.axis_size("aux")
    planes = pair_list.shape[0]
    width = virt // 4
    half = virt // 2
    slices = next(n for n in (5, 3, 2, 1) if local_q % (16 * n) == 0)
    rows = local_q // slices
    steps = planes * slices
    aux = lax.axis_index("aux")
    occ = lax.axis_index("occ")
    z, x, y, c = aux // 2, aux % 2, occ // 2, occ % 2

    chosen = lax.dynamic_index_in_dim(pair_list, z, 0, keepdims=False)
    e_i = lax.dynamic_index_in_dim(eps_occ, chosen[0] * orb_local + x, 0, keepdims=False)
    e_j = lax.dynamic_index_in_dim(eps_occ, chosen[1] * orb_local + y, 0, keepdims=False)
    halves = eps_virt.reshape(2, half)
    near = (halves - e_i - e_j).reshape(2, 1, half)
    far = jnp.where(c == 0, halves, halves[::-1]).reshape(2, half, 1)
    mine = factors.transpose(1, 0, 2)

    part, _, _ = pl.pallas_call(
        functools.partial(route, planes, slices),
        out_shape=[
            jax.ShapeDtypeStruct((2, 1, half), jnp.float32),
            jax.ShapeDtypeStruct((2, n_aux * local_q, virt), factors.dtype),
            jax.ShapeDtypeStruct((planes, 2, local_q, width), factors.dtype),
        ],
        in_specs=[
            pl.BlockSpec(memory_space=pltpu.SMEM),
            pl.BlockSpec(memory_space=pltpu.VMEM),
            pl.BlockSpec(memory_space=pltpu.VMEM),
            pl.BlockSpec(memory_space=pl.ANY),
        ],
        out_specs=[
            pl.BlockSpec(memory_space=pltpu.VMEM),
            pl.BlockSpec(memory_space=pl.ANY),
            pl.BlockSpec(memory_space=pl.ANY),
        ],
        scratch_shapes=[
            [pltpu.VMEM((4, 2, rows, width), factors.dtype) for _ in range(slices)],
            pltpu.VMEM((slices, planes, 2, 2, rows, width), factors.dtype),
            pltpu.VMEM((2, half, half), jnp.float32),
            pltpu.VMEM((2, 2, n_aux * rows, virt), factors.dtype),
            pltpu.VMEM((width, n_aux * rows), factors.dtype),
            pltpu.SemaphoreType.DMA((slices, 4)),
            pltpu.SemaphoreType.DMA((slices, 4)),
            pltpu.SemaphoreType.DMA((slices, planes, 2, 2)),
            pltpu.SemaphoreType.DMA((slices, planes, 2, 2)),
            pltpu.SemaphoreType.DMA((steps, 2, 3)),
            pltpu.SemaphoreType.DMA((steps, 2, 3)),
            pltpu.SemaphoreType.DMA((steps, 2, 4)),
            pltpu.SemaphoreType.DMA((steps, 2, 4)),
            pltpu.SemaphoreType.DMA((2, 2, n_aux)),
        ],
        compiler_params=pltpu.CompilerParams(
            collective_id=0, has_side_effects=True, vmem_limit_bytes=60 * 1024 * 1024
        ),
    )(pair_list, near, far, mine)

    spread = lax.all_to_all(part.reshape(n_aux, virt // n_aux), "aux", split_axis=0, concat_axis=0, tiled=True)
    every = lax.all_gather(spread, "occ", axis=0, tiled=False)
    every = every.reshape(2, 2, planes, 2, virt // n_aux).sum(axis=1)
    own = lax.dynamic_index_in_dim(every, occ, 1, keepdims=False)
    return own.transpose(1, 0, 2).reshape(1, 4, virt // n_aux)


def by_groups(factors, pair_list, eps_occ, eps_virt):
    local_q, orb_local, virt_width = factors.shape
    aux_count = lax.axis_size("aux")
    my_group = lax.axis_index("occ")
    chosen = pair_list[my_group]
    everyone = lax.all_gather(factors, "occ", axis=1, tiled=True)
    first_block = lax.dynamic_slice_in_dim(everyone, chosen[0] * orb_local, orb_local, 1)
    second = lax.dynamic_slice_in_dim(everyone, chosen[1] * orb_local, orb_local, 1)
    picked = jnp.stack([first_block, second], axis=0)
    rows_grid = 2 ** ((aux_count.bit_length() - 1) // 2)
    cols_grid = aux_count // rows_grid
    span_a = virt_width // rows_grid
    span_b = virt_width // cols_grid
    rows_pieces = picked.reshape(2, local_q, orb_local, rows_grid, span_a).transpose(3, 0, 1, 2, 4)
    rows_pieces = jnp.tile(rows_pieces, (cols_grid, 1, 1, 1, 1))
    cols_pieces = picked.reshape(2, local_q, orb_local, cols_grid, span_b).transpose(3, 0, 1, 2, 4)
    cols_pieces = jnp.repeat(cols_pieces, rows_grid, axis=0)
    send_pieces = jnp.concatenate([rows_pieces, cols_pieces], axis=4)
    regrouped = lax.all_to_all(send_pieces, "aux", split_axis=0, concat_axis=2, tiled=True)[0]
    aux_rank = lax.axis_index("aux")
    row_id = aux_rank % rows_grid
    col_id = aux_rank // rows_grid
    contract = (((0,), (0,)), ((), ()))
    direct = lax.dot_general(
        regrouped[0, :, :, :span_a], regrouped[1, :, :, span_a:], contract, preferred_element_type=jnp.float32
    )
    swapped = lax.dot_general(
        regrouped[1, :, :, :span_a], regrouped[0, :, :, span_a:], contract, preferred_element_type=jnp.float32
    )
    swapped = swapped.transpose(2, 1, 0, 3)
    virt_rows = lax.dynamic_slice_in_dim(eps_virt, row_id * span_a, span_a)
    virt_cols = lax.dynamic_slice_in_dim(eps_virt, col_id * span_b, span_b)
    occ_left = lax.dynamic_slice_in_dim(eps_occ, chosen[0] * orb_local, orb_local)
    occ_right = lax.dynamic_slice_in_dim(eps_occ, chosen[1] * orb_local, orb_local)
    denominator = (
        virt_rows[None, :, None, None]
        + virt_cols[None, None, None, :]
        - occ_left[:, None, None, None]
        - occ_right[None, None, :, None]
    )
    partial_value = -jnp.sum(direct * (2.0 * direct - swapped) / denominator, axis=3)
    partial_value = partial_value.transpose(0, 2, 1).reshape(orb_local * orb_local, span_a)
    spread = lax.dynamic_update_slice_in_dim(
        jnp.zeros((orb_local * orb_local, virt_width), jnp.float32), partial_value, row_id * span_a, 1
    )
    shares = lax.psum_scatter(spread, "aux", scatter_dimension=1, tiled=True)
    return shares.reshape(1, orb_local * orb_local, -1)


def solution(mesh):
    def on_device(factors, pair_list, eps_occ, eps_virt):
        planes = pair_list.shape[0]
        fits = (
            mesh.shape["aux"] == 2 * planes
            and mesh.shape["occ"] == 4
            and planes == 4
            and factors.shape[1] == 2
            and factors.shape[0] % 16 == 0
            and factors.shape[2] % 512 == 0
        )
        body = by_planes if fits else by_groups
        return body(factors, pair_list, eps_occ, eps_virt)

    return jax.shard_map(
        on_device,
        mesh=mesh,
        in_specs=(P("aux", "occ", None), P(), P(), P()),
        out_specs=P("occ", None, "aux"),
        check_vma=False,
    )
```

```python
import functools

import jax
import jax.numpy as jnp
from jax import lax
from jax.experimental import pallas as pl
from jax.experimental.pallas import tpu as pltpu
from jax.sharding import PartitionSpec as P

MESH = pl.DeviceIdType.MESH


def flip(z, k):
    return (z // 2 + k // 2) % 2 * 2 + (z + k) % 2


def route(
    planes, slices, pairs, e_occ, e_virt, mine, every, gath, zbuf, quarter, sel, acc, rec, held, turned, part,
    fin_send, fin_recv, o_send, o_recv, z_send, z_recv, hop_send, hop_recv, core_send, core_recv, held_sem,
):
    depth, virt = mine.shape[1], mine.shape[2]
    rows = depth // slices
    width = virt // 4
    half = virt // 2
    steps = planes * slices
    aux = lax.axis_index("aux")
    occ = lax.axis_index("occ")
    z, x, y, c = aux // 2, aux % 2, occ // 2, occ % 2

    def device(z_, x_, y_, c_):
        return {"aux": z_ * 2 + x_, "occ": y_ * 2 + c_}

    def fellow(d):
        return {"aux": aux, "occ": flip(occ, d)}

    def source(m):
        return device(occ, m // 4, m // 2 % 2, m % 2)

    def is_me(m):
        return (occ == z) & (m == x * 4 + y * 2 + c)

    partners = [device(flip(z, k), x, y, c) for k in range(1, planes)]
    partners += [fellow(d) for d in range(1, 4)] + [device(z, 1 - x, y, c)]
    barrier = pltpu.get_barrier_semaphore()
    for partner in partners:
        pl.semaphore_signal(barrier, inc=1, device_id=partner, device_id_type=MESH)
    for m in range(8):

        @pl.when(jnp.logical_not(is_me(m)))
        def _():
            pl.semaphore_signal(barrier, inc=1, device_id=source(m), device_id_type=MESH)

    pl.semaphore_wait(barrier, len(partners) + 8 - jnp.where(z == occ, 1, 0))

    def span(t):
        return pl.ds(pl.multiple_of(t * rows, 16), rows)

    def place(s, zs, xs, ys, cs, t):
        first = pl.multiple_of((zs * 2 + xs) * depth + t * rows, 16)
        left = pl.multiple_of((ys * 2 + cs) * width, 128)
        return gath.at[s, pl.ds(first, rows), pl.ds(left, width)]

    def o_copy(t, d):
        to = flip(occ, d)
        src = mine.at[:, pl.ds(t * rows, rows), pl.ds(pl.multiple_of(to * width, 128), width)]
        if d == 0:
            return pltpu.make_async_copy(src, quarter[t].at[occ], o_recv.at[t, 0])
        return pltpu.make_async_remote_copy(
            src_ref=src,
            dst_ref=quarter[t].at[occ],
            send_sem=o_send.at[t, d],
            recv_sem=o_recv.at[t, d],
            device_id=fellow(d),
            device_id_type=MESH,
        )

    def z_copy(t, k, s, rel):
        zt = flip(z, k)
        own = x if s == 0 else y
        w = own if rel == 0 else 1 - own
        dst = place(s, z, x, y, c, t) if rel == 0 else zbuf.at[k, s, span(t), :]
        return pltpu.make_async_remote_copy(
            src_ref=sel.at[t, zt, s, w],
            dst_ref=dst,
            send_sem=z_send.at[t, k, s, rel],
            recv_sem=z_recv.at[t, k, s, rel],
            device_id=device(zt, x, y, c),
            device_id_type=MESH,
        )

    def z_keep(t, s, rel):
        own = x if s == 0 else y
        w = own if rel == 0 else 1 - own
        dst = place(s, z, x, y, c, t) if rel == 0 else zbuf.at[0, s, span(t), :]
        return pltpu.make_async_copy(sel.at[t, z, s, w], dst, z_recv.at[t, 0, s, rel])

    def hop(n, s, kind):
        t, k = n // planes, n % planes
        zs = flip(z, k)
        share = device(z, x, 1 - y, c) if s == 0 else device(z, 1 - x, y, c)
        other = device(z, 1 - x, y, c) if s == 0 else device(z, x, 1 - y, c)
        xs, ys = (1 - x, y) if s == 0 else (x, 1 - y)
        own = place(s, zs, x, y, c, t)
        if kind == 0:
            src, dst, target = own, own, share
        elif kind == 1:
            src, dst, target = zbuf.at[k, s, span(t), :], own, other
        else:
            src = place(s, zs, xs, ys, c, t)
            dst, target = src, share
        return pltpu.make_async_remote_copy(
            src_ref=src,
            dst_ref=dst,
            send_sem=hop_send.at[n, s, kind],
            recv_sem=hop_recv.at[n, s, kind],
            device_id=target,
            device_id_type=MESH,
        )

    def across(n, s, kind):
        t, k = n // planes, n % planes
        zs = flip(z, k)
        if s == 0:
            spots = [(x, y), (x, 1 - y), (1 - x, y), (1 - x, 1 - y)]
        else:
            spots = [(x, y), (1 - x, y), (x, 1 - y), (1 - x, 1 - y)]
        ref = place(s, zs, spots[kind][0], spots[kind][1], c, t)
        return pltpu.make_async_remote_copy(
            src_ref=ref,
            dst_ref=ref,
            send_sem=core_send.at[n, s, kind],
            recv_sem=core_recv.at[n, s, kind],
            device_id=device(z, x, y, 1 - c),
            device_id_type=MESH,
        )

    def fetch(t, s, q):
        first = pl.multiple_of(q * depth + t * rows, 16)
        return pltpu.make_async_copy(
            gath.at[s, pl.ds(first, rows), :],
            held.at[t % 2, s, pl.ds(q * rows, rows), :],
            held_sem.at[t % 2, s, q],
        )

    def start_exchange(t):
        for d in (2, 3, 1, 0):
            o_copy(t, d).start()

    def choose(t):
        for d in (0, 1, 2, 3):
            if d == 0:
                o_copy(t, d).wait()
            else:
                o_copy(t, d).wait_recv()
        for p in range(planes):
            for s in range(2):
                block = pairs[p, s]
                for w in range(2):
                    sel[t, p, s, w] = quarter[t][block, w]
        for s in range(2):
            for rel in (1, 0):
                z_keep(t, s, rel).start()
                for k in (2, 3, 1):
                    z_copy(t, k, s, rel).start()

    def last(a):
        return pltpu.make_async_remote_copy(
            src_ref=part,
            dst_ref=every.at[x * 4 + y * 2 + c],
            send_sem=fin_send.at[a],
            recv_sem=fin_recv.at[x * 4 + y * 2 + c],
            device_id={"aux": a, "occ": z},
            device_id_type=MESH,
        )

    def last_keep():
        m = x * 4 + y * 2 + c
        return pltpu.make_async_copy(part, every.at[m], fin_recv.at[m])

    def last_from(m):
        return pltpu.make_async_remote_copy(
            src_ref=part,
            dst_ref=every.at[m],
            send_sem=fin_send.at[m],
            recv_sem=fin_recv.at[m],
            device_id=source(m),
            device_id_type=MESH,
        )

    for t in range(min(2, slices)):
        start_exchange(t)

    e_i = e_occ[pairs[z, 0] * 2 + x]
    e_j = e_occ[pairs[z, 1] * 2 + y]

    @pl.loop(0, 2 * (half // 128))
    def _(r):
        tile, blk = r // (half // 128), r % (half // 128)
        acc[tile, pl.ds(pl.multiple_of(blk * 128, 128), 128), :] = jnp.zeros((128, half), jnp.float32)

    @pl.loop(0, 2 * (half // 128))
    def _(r):
        tile, blk = r // (half // 128), r % (half // 128)
        at = pl.ds(pl.multiple_of(blk * 128, 128), 128)
        first = pl.multiple_of((tile + c) % 2 * half + blk * 128, 128)
        far = jnp.broadcast_to(e_virt[:, pl.ds(first, 128)], (128, 128)).T
        for g in range(half // 128):
            near = e_virt[:, pl.ds(pl.multiple_of(tile * half + g * 128, 128), 128)]
            rec[tile, at, g * 128 : (g + 1) * 128] = 1.0 / (near + far - e_i - e_j)

    choose(0)
    for t in range(2, min(4, slices)):
        start_exchange(t)
    if slices > 1:
        choose(1)
    for t in range(4, slices):
        start_exchange(t)

    @pl.loop(0, steps + 8)
    def _(n):
        for t in range(2, slices):

            @pl.when(n == planes * (t - 2))
            def _():
                choose(t)

        @pl.when(n < steps)
        def _():
            t, k = n // planes, n % planes
            for s in range(2):
                for rel in (1, 0):

                    @pl.when(k == 0)
                    def _():
                        z_keep(t, s, rel).wait()

                    @pl.when(k > 0)
                    def _():
                        z_copy(t, k, s, rel).wait_recv()

                    hop(n, s, rel).start()
                    if rel == 0:
                        across(n, s, 0).start()

        @pl.when((n >= 1) & (n < steps + 1))
        def _():
            for s in range(2):
                hop(n - 1, s, 1).wait_recv()
                hop(n - 1, s, 2).start()
                across(n - 1, s, 2).start()

        @pl.when((n >= 2) & (n < steps + 2))
        def _():
            for s in range(2):
                hop(n - 2, s, 0).wait_recv()
                across(n - 2, s, 1).start()
                hop(n - 2, s, 2).wait_recv()
                across(n - 2, s, 3).start()

        @pl.when((n >= 3) & (n < steps + 3))
        def _():
            for s in range(2):
                for kind in range(4):
                    across(n - 3, s, kind).wait_recv()

        @pl.when((n >= 6) & (n < steps + 6) & (n % planes == 2))
        def _():
            t = (n - 6) // planes
            for s in range(2):
                for q in range(2 * planes):
                    fetch(t, s, q).start()

        @pl.when(n >= 8)
        def _():
            t, unit = (n - 8) // planes, n % planes

            @pl.when(unit == 0)
            def _():
                for s in range(2):
                    for q in range(2 * planes):
                        fetch(t, s, q).wait()

            tile = unit // 2
            top = pl.multiple_of(unit % 2 * width, 128)
            left = pl.multiple_of((tile + c) % 2 * half, 128)
            lhs = pl.multiple_of(tile * half + unit % 2 * width, 128)
            turned[...] = held[t % 2, 0, :, pl.ds(lhs, width)].T

            @pl.loop(0, half // 256)
            def _(col):
                cols = pl.ds(pl.multiple_of(left + col * 256, 128), 256)
                into = pl.ds(pl.multiple_of(col * 256, 128), 256)
                acc[tile, pl.ds(top, width), into] += jnp.dot(
                    turned[...], held[t % 2, 1, :, cols], preferred_element_type=jnp.float32
                )

    @pl.loop(0, 2 * (half // 128))
    def _(r):
        tile, blk = r // (half // 128), r % (half // 128)
        at = pl.ds(pl.multiple_of(blk * 128, 128), 128)
        direct = acc[tile, at, :].T
        swapped = acc[(tile + c) % 2, :, at]
        value = direct * (2.0 * direct - swapped) * rec[tile, :, at]
        part[tile, :, at] = -jnp.sum(value, axis=0, keepdims=True)

    def to_me(a):
        return (z == occ) & (a == aux)

    for a in range(8):

        @pl.when(to_me(a))
        def _():
            last_keep().start()

        @pl.when(jnp.logical_not(to_me(a)))
        def _():
            last(a).start()

    for t in range(slices):
        for d in (1, 2, 3):
            o_copy(t, d).wait_send()

    @pl.loop(0, slices)
    def _(t):
        for s in range(2):
            for rel in (1, 0):
                for k in (2, 3, 1):
                    z_copy(t, k, s, rel).wait_send()

    @pl.loop(0, steps)
    def _(n):
        for s in range(2):
            for kind in range(3):
                hop(n, s, kind).wait_send()
            for kind in range(4):
                across(n, s, kind).wait_send()

    for m in range(8):

        @pl.when(is_me(m))
        def _():
            last_keep().wait()

        @pl.when(jnp.logical_not(is_me(m)))
        def _():
            last_from(m).wait_recv()

    for a in range(8):

        @pl.when(jnp.logical_not(to_me(a)))
        def _():
            last(a).wait_send()


def by_planes(factors, pair_list, eps_occ, eps_virt):
    local_q, orb_local, virt = factors.shape
    n_aux = lax.axis_size("aux")
    planes = pair_list.shape[0]
    width = virt // 4
    half = virt // 2
    slices = next(n for n in (5, 3, 2, 1) if local_q % (16 * n) == 0)
    rows = local_q // slices
    steps = planes * slices
    aux = lax.axis_index("aux")
    mine = factors.transpose(1, 0, 2)

    every, _, _ = pl.pallas_call(
        functools.partial(route, planes, slices),
        out_shape=[
            jax.ShapeDtypeStruct((8, 2, 1, half), jnp.float32),
            jax.ShapeDtypeStruct((2, n_aux * local_q, virt), factors.dtype),
            jax.ShapeDtypeStruct((planes, 2, local_q, width), factors.dtype),
        ],
        in_specs=[
            pl.BlockSpec(memory_space=pltpu.SMEM),
            pl.BlockSpec(memory_space=pltpu.SMEM),
            pl.BlockSpec(memory_space=pltpu.VMEM),
            pl.BlockSpec(memory_space=pl.ANY),
        ],
        out_specs=[
            pl.BlockSpec(memory_space=pltpu.VMEM),
            pl.BlockSpec(memory_space=pl.ANY),
            pl.BlockSpec(memory_space=pl.ANY),
        ],
        scratch_shapes=[
            [pltpu.VMEM((4, 2, rows, width), factors.dtype) for _ in range(slices)],
            pltpu.VMEM((slices, planes, 2, 2, rows, width), factors.dtype),
            pltpu.VMEM((2, half, half), jnp.float32),
            pltpu.VMEM((2, half, half), jnp.float32),
            pltpu.VMEM((2, 2, n_aux * rows, virt), factors.dtype),
            pltpu.VMEM((width, n_aux * rows), factors.dtype),
            pltpu.VMEM((2, 1, half), jnp.float32),
            pltpu.SemaphoreType.DMA((8,)),
            pltpu.SemaphoreType.DMA((8,)),
            pltpu.SemaphoreType.DMA((slices, 4)),
            pltpu.SemaphoreType.DMA((slices, 4)),
            pltpu.SemaphoreType.DMA((slices, planes, 2, 2)),
            pltpu.SemaphoreType.DMA((slices, planes, 2, 2)),
            pltpu.SemaphoreType.DMA((steps, 2, 3)),
            pltpu.SemaphoreType.DMA((steps, 2, 3)),
            pltpu.SemaphoreType.DMA((steps, 2, 4)),
            pltpu.SemaphoreType.DMA((steps, 2, 4)),
            pltpu.SemaphoreType.DMA((2, 2, n_aux)),
        ],
        compiler_params=pltpu.CompilerParams(
            collective_id=0, has_side_effects=True, vmem_limit_bytes=60 * 1024 * 1024
        ),
    )(pair_list, eps_occ, eps_virt.reshape(1, virt), mine)

    totals = every.reshape(4, 2, virt).sum(axis=1)
    return lax.dynamic_slice_in_dim(totals, aux * (virt // n_aux), virt // n_aux, 1)[None]


def by_groups(factors, pair_list, eps_occ, eps_virt):
    local_q, orb_local, virt_width = factors.shape
    aux_count = lax.axis_size("aux")
    my_group = lax.axis_index("occ")
    chosen = pair_list[my_group]
    everyone = lax.all_gather(factors, "occ", axis=1, tiled=True)
    first_block = lax.dynamic_slice_in_dim(everyone, chosen[0] * orb_local, orb_local, 1)
    second = lax.dynamic_slice_in_dim(everyone, chosen[1] * orb_local, orb_local, 1)
    picked = jnp.stack([first_block, second], axis=0)
    rows_grid = 2 ** ((aux_count.bit_length() - 1) // 2)
    cols_grid = aux_count // rows_grid
    span_a = virt_width // rows_grid
    span_b = virt_width // cols_grid
    rows_pieces = picked.reshape(2, local_q, orb_local, rows_grid, span_a).transpose(3, 0, 1, 2, 4)
    rows_pieces = jnp.tile(rows_pieces, (cols_grid, 1, 1, 1, 1))
    cols_pieces = picked.reshape(2, local_q, orb_local, cols_grid, span_b).transpose(3, 0, 1, 2, 4)
    cols_pieces = jnp.repeat(cols_pieces, rows_grid, axis=0)
    send_pieces = jnp.concatenate([rows_pieces, cols_pieces], axis=4)
    regrouped = lax.all_to_all(send_pieces, "aux", split_axis=0, concat_axis=2, tiled=True)[0]
    aux_rank = lax.axis_index("aux")
    row_id = aux_rank % rows_grid
    col_id = aux_rank // rows_grid
    contract = (((0,), (0,)), ((), ()))
    direct = lax.dot_general(
        regrouped[0, :, :, :span_a], regrouped[1, :, :, span_a:], contract, preferred_element_type=jnp.float32
    )
    swapped = lax.dot_general(
        regrouped[1, :, :, :span_a], regrouped[0, :, :, span_a:], contract, preferred_element_type=jnp.float32
    )
    swapped = swapped.transpose(2, 1, 0, 3)
    virt_rows = lax.dynamic_slice_in_dim(eps_virt, row_id * span_a, span_a)
    virt_cols = lax.dynamic_slice_in_dim(eps_virt, col_id * span_b, span_b)
    occ_left = lax.dynamic_slice_in_dim(eps_occ, chosen[0] * orb_local, orb_local)
    occ_right = lax.dynamic_slice_in_dim(eps_occ, chosen[1] * orb_local, orb_local)
    denominator = (
        virt_rows[None, :, None, None]
        + virt_cols[None, None, None, :]
        - occ_left[:, None, None, None]
        - occ_right[None, None, :, None]
    )
    partial_value = -jnp.sum(direct * (2.0 * direct - swapped) / denominator, axis=3)
    partial_value = partial_value.transpose(0, 2, 1).reshape(orb_local * orb_local, span_a)
    spread = lax.dynamic_update_slice_in_dim(
        jnp.zeros((orb_local * orb_local, virt_width), jnp.float32), partial_value, row_id * span_a, 1
    )
    shares = lax.psum_scatter(spread, "aux", scatter_dimension=1, tiled=True)
    return shares.reshape(1, orb_local * orb_local, -1)


def solution(mesh):
    def on_device(factors, pair_list, eps_occ, eps_virt):
        planes = pair_list.shape[0]
        fits = (
            mesh.shape["aux"] == 2 * planes
            and mesh.shape["occ"] == 4
            and planes == 4
            and factors.shape[1] == 2
            and factors.shape[0] % 16 == 0
            and factors.shape[2] % 512 == 0
        )
        body = by_planes if fits else by_groups
        return body(factors, pair_list, eps_occ, eps_virt)

    return jax.shard_map(
        on_device,
        mesh=mesh,
        in_specs=(P("aux", "occ", None), P(), P(), P()),
        out_specs=P("occ", None, "aux"),
        check_vma=False,
    )
```

```python
import functools

import jax
import jax.numpy as jnp
from jax import lax
from jax.experimental import pallas as pl
from jax.experimental.pallas import tpu as pltpu
from jax.sharding import PartitionSpec as P

MESH = pl.DeviceIdType.MESH


def flip(z, k):
    return (z // 2 + k // 2) % 2 * 2 + (z + k) % 2


def route(
    planes, slices, pairs, e_occ, e_virt, mine, every, gath, zbuf, quarter, sel, acc, rec, held, turned, part,
    fin_send, fin_recv, o_send, o_recv, z_send, z_recv, hop_send, hop_recv, core_send, core_recv, held_sem,
):
    depth, virt = mine.shape[1], mine.shape[2]
    rows = depth // slices
    width = virt // 4
    half = virt // 2
    steps = 2 * planes * slices
    aux = lax.axis_index("aux")
    occ = lax.axis_index("occ")
    z, x, y, c = aux // 2, aux % 2, occ // 2, occ % 2

    def device(z_, x_, y_, c_):
        return {"aux": z_ * 2 + x_, "occ": y_ * 2 + c_}

    def fellow(d):
        return {"aux": aux, "occ": flip(occ, d)}

    def source(m):
        return device(occ, m // 4, m // 2 % 2, m % 2)

    def is_me(m):
        return (occ == z) & (m == x * 4 + y * 2 + c)

    partners = [device(flip(z, k), x, y, c) for k in range(1, planes)]
    partners += [fellow(d) for d in range(1, 4)] + [device(z, 1 - x, y, c)]
    barrier = pltpu.get_barrier_semaphore()
    for partner in partners:
        pl.semaphore_signal(barrier, inc=1, device_id=partner, device_id_type=MESH)
    for m in range(8):

        @pl.when(jnp.logical_not(is_me(m)))
        def _():
            pl.semaphore_signal(barrier, inc=1, device_id=source(m), device_id_type=MESH)

    pl.semaphore_wait(barrier, len(partners) + 8 - jnp.where(z == occ, 1, 0))

    def span(t):
        return pl.ds(pl.multiple_of(t * rows, 16), rows)

    def place(s, zs, xs, ys, cs, t):
        left = pl.multiple_of((cs * 2 + ys) * width, 128)
        return gath.at[s, zs, xs, span(t), pl.ds(left, width)]

    def o_copy(t, d):
        to = flip(occ, d)
        left = pl.multiple_of((to % 2 * 2 + to // 2) * width, 128)
        src = mine.at[:, pl.ds(t * rows, rows), pl.ds(left, width)]
        if d == 0:
            return pltpu.make_async_copy(src, quarter[t].at[occ], o_recv.at[t, 0])
        return pltpu.make_async_remote_copy(
            src_ref=src,
            dst_ref=quarter[t].at[occ],
            send_sem=o_send.at[t, d],
            recv_sem=o_recv.at[t, d],
            device_id=fellow(d),
            device_id_type=MESH,
        )

    def z_copy(t, k, s, rel):
        zt = flip(z, k)
        own = x * (1 - s) + y * s
        w = own if rel == 0 else 1 - own
        dst = place(s, z, x, y, c, t) if rel == 0 else zbuf.at[k, s, span(t), :]
        return pltpu.make_async_remote_copy(
            src_ref=sel.at[t, zt, s, w],
            dst_ref=dst,
            send_sem=z_send.at[t, k, s, rel],
            recv_sem=z_recv.at[t, k, s, rel],
            device_id=device(zt, x, y, c),
            device_id_type=MESH,
        )

    def z_keep(t, s, rel):
        own = x * (1 - s) + y * s
        w = own if rel == 0 else 1 - own
        dst = place(s, z, x, y, c, t) if rel == 0 else zbuf.at[0, s, span(t), :]
        return pltpu.make_async_copy(sel.at[t, z, s, w], dst, z_recv.at[t, 0, s, rel])

    def parts_of(n):
        j = n % planes
        return n // (2 * planes), n // planes % 2, jnp.minimum(j, 1) * (1 + j % 3)

    def hop(n, kind):
        t, s, k = parts_of(n)
        zs = flip(z, k)
        xf, yf = x + s * (1 - 2 * x), y + (1 - s) * (1 - 2 * y)
        xo, yo = x + (1 - s) * (1 - 2 * x), y + s * (1 - 2 * y)
        share, other = device(z, xf, yf, c), device(z, xo, yo, c)
        own = place(s, zs, x, y, c, t)
        if kind == 0:
            src, dst, target = own, own, share
        elif kind == 1:
            src, dst, target = zbuf.at[k, s, span(t), :], own, other
        else:
            src = place(s, zs, xo, yo, c, t)
            dst, target = src, share
        return pltpu.make_async_remote_copy(
            src_ref=src,
            dst_ref=dst,
            send_sem=hop_send.at[n, kind],
            recv_sem=hop_recv.at[n, kind],
            device_id=target,
            device_id_type=MESH,
        )

    def across(n):
        t, s, k = parts_of(n)
        ref = gath.at[s, flip(z, k), :, span(t), pl.ds(pl.multiple_of(c * half, 128), half)]
        return pltpu.make_async_remote_copy(
            src_ref=ref,
            dst_ref=ref,
            send_sem=core_send.at[n],
            recv_sem=core_recv.at[n],
            device_id=device(z, x, y, 1 - c),
            device_id_type=MESH,
        )

    def fetch(t, s):
        return pltpu.make_async_copy(gath.at[s, :, :, span(t), :], held.at[t % 2, s], held_sem.at[t % 2, s])

    def start_exchange(t):
        for d in (2, 3, 1, 0):
            o_copy(t, d).start()

    def choose(t):
        for d in (0, 1, 2, 3):
            if d == 0:
                o_copy(t, d).wait()
            else:
                o_copy(t, d).wait_recv()
        for p in range(planes):
            for s in range(2):
                block = pairs[p, s]
                for w in range(2):
                    sel[t, p, s, w] = quarter[t][block, w]
        for s in range(2):
            for rel in (1, 0):
                z_keep(t, s, rel).start()
            for k in (2, 3, 1):
                for rel in (1, 0):
                    z_copy(t, k, s, rel).start()

    def last(a):
        return pltpu.make_async_remote_copy(
            src_ref=part,
            dst_ref=every.at[x * 4 + y * 2 + c],
            send_sem=fin_send.at[a],
            recv_sem=fin_recv.at[x * 4 + y * 2 + c],
            device_id={"aux": a, "occ": z},
            device_id_type=MESH,
        )

    def last_keep():
        m = x * 4 + y * 2 + c
        return pltpu.make_async_copy(part, every.at[m], fin_recv.at[m])

    def last_from(m):
        return pltpu.make_async_remote_copy(
            src_ref=part,
            dst_ref=every.at[m],
            send_sem=fin_send.at[m],
            recv_sem=fin_recv.at[m],
            device_id=source(m),
            device_id_type=MESH,
        )

    for t in range(min(2, slices)):
        start_exchange(t)

    e_i = e_occ[pairs[z, 0] * 2 + x]
    e_j = e_occ[pairs[z, 1] * 2 + y]

    choose(0)
    for t in range(2, min(4, slices)):
        start_exchange(t)

    @pl.loop(0, 2 * (half // 128))
    def _(r):
        tile, blk = r // (half // 128), r % (half // 128)
        acc[tile, pl.ds(pl.multiple_of(blk * 128, 128), 128), :] = jnp.zeros((128, half), jnp.float32)

    @pl.loop(0, 2 * (half // 128))
    def _(r):
        tile, blk = r // (half // 128), r % (half // 128)
        at = pl.ds(pl.multiple_of(blk * 128, 128), 128)
        first = pl.multiple_of((tile + c) % 2 * half + blk * 128, 128)
        far = jnp.broadcast_to(e_virt[:, pl.ds(first, 128)], (128, 128)).T
        for g in range(half // 128):
            near = e_virt[:, pl.ds(pl.multiple_of(tile * half + g * 128, 128), 128)]
            rec[tile, at, g * 128 : (g + 1) * 128] = 1.0 / (near + far - e_i - e_j)

    if slices > 1:
        choose(1)
    for t in range(4, min(6, slices)):
        start_exchange(t)

    @pl.loop(0, steps + 12)
    def _(n):
        for t in range(2, slices):

            @pl.when(n == 2 * planes * (t - 2))
            def _():
                choose(t)
                if t + 4 < slices:
                    start_exchange(t + 4)

        @pl.when(n < steps)
        def _():
            t, s, k = parts_of(n)
            for rel in (1, 0):

                @pl.when(k == 0)
                def _():
                    z_keep(t, s, rel).wait()

                @pl.when(k > 0)
                def _():
                    z_copy(t, k, s, rel).wait_recv()

                hop(n, rel).start()

        @pl.when((n >= 1) & (n < steps + 1))
        def _():
            hop(n - 1, 1).wait_recv()
            hop(n - 1, 2).start()

        @pl.when((n >= 2) & (n < steps + 2))
        def _():
            hop(n - 2, 0).wait_recv()
            hop(n - 2, 2).wait_recv()
            across(n - 2).start()

        @pl.when((n >= 3) & (n < steps + 3))
        def _():
            across(n - 3).wait_recv()

        @pl.when((n >= 10) & (n < steps + 10) & (n % 8 == 2))
        def _():
            for s in range(2):
                fetch((n - 10) // 8, s).start()

        @pl.when((n >= 12) & (n % 2 == 0))
        def _():
            t, unit = (n - 12) // 8, (n - 12) % 8 // 2

            @pl.when(unit == 0)
            def _():
                for s in range(2):
                    fetch(t, s).wait()

            tile = unit // 2
            top = pl.multiple_of(unit % 2 * width, 128)
            left = pl.multiple_of((tile + c) % 2 * half, 128)
            lhs = pl.multiple_of(tile * half + unit % 2 * width, 128)
            turned[...] = held[t % 2, 0, :, :, :, pl.ds(lhs, width)].reshape(2 * planes * rows, width).T

            @pl.loop(0, half // 256)
            def _(col):
                cols = pl.ds(pl.multiple_of(left + col * 256, 128), 256)
                into = pl.ds(pl.multiple_of(col * 256, 128), 256)
                acc[tile, pl.ds(top, width), into] += jnp.dot(
                    turned[...],
                    held[t % 2, 1, :, :, :, cols].reshape(2 * planes * rows, 256),
                    preferred_element_type=jnp.float32,
                )

    @pl.loop(0, 2 * (half // 128))
    def _(r):
        tile, blk = r // (half // 128), r % (half // 128)
        at = pl.ds(pl.multiple_of(blk * 128, 128), 128)
        direct = acc[tile, at, :].T
        swapped = acc[(tile + c) % 2, :, at]
        value = direct * (2.0 * direct - swapped) * rec[tile, :, at]
        part[tile, :, at] = -jnp.sum(value, axis=0, keepdims=True)

    def to_me(a):
        return (z == occ) & (a == aux)

    for a in range(8):

        @pl.when(to_me(a))
        def _():
            last_keep().start()

        @pl.when(jnp.logical_not(to_me(a)))
        def _():
            last(a).start()

    for t in range(slices):
        for d in (1, 2, 3):
            o_copy(t, d).wait_send()

    @pl.loop(0, slices)
    def _(t):
        for s in range(2):
            for rel in (1, 0):
                for k in (2, 3, 1):
                    z_copy(t, k, s, rel).wait_send()

    @pl.loop(0, steps)
    def _(n):
        for kind in range(3):
            hop(n, kind).wait_send()
        across(n).wait_send()

    for m in range(8):

        @pl.when(is_me(m))
        def _():
            last_keep().wait()

        @pl.when(jnp.logical_not(is_me(m)))
        def _():
            last_from(m).wait_recv()

    for a in range(8):

        @pl.when(jnp.logical_not(to_me(a)))
        def _():
            last(a).wait_send()


def by_planes(factors, pair_list, eps_occ, eps_virt):
    local_q, orb_local, virt = factors.shape
    n_aux = lax.axis_size("aux")
    planes = pair_list.shape[0]
    width = virt // 4
    half = virt // 2
    slices = next(n for n in (10, 5, 3, 2, 1) if local_q % (16 * n) == 0)
    rows = local_q // slices
    steps = 2 * planes * slices
    aux = lax.axis_index("aux")
    mine = factors.transpose(1, 0, 2)

    every, _, _ = pl.pallas_call(
        functools.partial(route, planes, slices),
        out_shape=[
            jax.ShapeDtypeStruct((8, 2, 1, half), jnp.float32),
            jax.ShapeDtypeStruct((2, planes, 2, local_q, virt), factors.dtype),
            jax.ShapeDtypeStruct((planes, 2, local_q, width), factors.dtype),
        ],
        in_specs=[
            pl.BlockSpec(memory_space=pltpu.SMEM),
            pl.BlockSpec(memory_space=pltpu.SMEM),
            pl.BlockSpec(memory_space=pltpu.VMEM),
            pl.BlockSpec(memory_space=pl.ANY),
        ],
        out_specs=[
            pl.BlockSpec(memory_space=pltpu.VMEM),
            pl.BlockSpec(memory_space=pl.ANY),
            pl.BlockSpec(memory_space=pl.ANY),
        ],
        scratch_shapes=[
            [pltpu.VMEM((4, 2, rows, width), factors.dtype) for _ in range(slices)],
            pltpu.VMEM((slices, planes, 2, 2, rows, width), factors.dtype),
            pltpu.VMEM((2, half, half), jnp.float32),
            pltpu.VMEM((2, half, half), jnp.float32),
            pltpu.VMEM((2, 2, planes, 2, rows, virt), factors.dtype),
            pltpu.VMEM((width, n_aux * rows), factors.dtype),
            pltpu.VMEM((2, 1, half), jnp.float32),
            pltpu.SemaphoreType.DMA((8,)),
            pltpu.SemaphoreType.DMA((8,)),
            pltpu.SemaphoreType.DMA((slices, 4)),
            pltpu.SemaphoreType.DMA((slices, 4)),
            pltpu.SemaphoreType.DMA((slices, planes, 2, 2)),
            pltpu.SemaphoreType.DMA((slices, planes, 2, 2)),
            pltpu.SemaphoreType.DMA((steps, 3)),
            pltpu.SemaphoreType.DMA((steps, 3)),
            pltpu.SemaphoreType.DMA((steps,)),
            pltpu.SemaphoreType.DMA((steps,)),
            pltpu.SemaphoreType.DMA((2, 2)),
        ],
        compiler_params=pltpu.CompilerParams(
            collective_id=0, has_side_effects=True, vmem_limit_bytes=60 * 1024 * 1024
        ),
    )(pair_list, eps_occ, eps_virt.reshape(1, virt), mine)

    totals = every.reshape(4, 2, virt).sum(axis=1)
    return lax.dynamic_slice_in_dim(totals, aux * (virt // n_aux), virt // n_aux, 1)[None]


def by_groups(factors, pair_list, eps_occ, eps_virt):
    local_q, orb_local, virt_width = factors.shape
    aux_count = lax.axis_size("aux")
    my_group = lax.axis_index("occ")
    chosen = pair_list[my_group]
    everyone = lax.all_gather(factors, "occ", axis=1, tiled=True)
    first_block = lax.dynamic_slice_in_dim(everyone, chosen[0] * orb_local, orb_local, 1)
    second = lax.dynamic_slice_in_dim(everyone, chosen[1] * orb_local, orb_local, 1)
    picked = jnp.stack([first_block, second], axis=0)
    rows_grid = 2 ** ((aux_count.bit_length() - 1) // 2)
    cols_grid = aux_count // rows_grid
    span_a = virt_width // rows_grid
    span_b = virt_width // cols_grid
    rows_pieces = picked.reshape(2, local_q, orb_local, rows_grid, span_a).transpose(3, 0, 1, 2, 4)
    rows_pieces = jnp.tile(rows_pieces, (cols_grid, 1, 1, 1, 1))
    cols_pieces = picked.reshape(2, local_q, orb_local, cols_grid, span_b).transpose(3, 0, 1, 2, 4)
    cols_pieces = jnp.repeat(cols_pieces, rows_grid, axis=0)
    send_pieces = jnp.concatenate([rows_pieces, cols_pieces], axis=4)
    regrouped = lax.all_to_all(send_pieces, "aux", split_axis=0, concat_axis=2, tiled=True)[0]
    aux_rank = lax.axis_index("aux")
    row_id = aux_rank % rows_grid
    col_id = aux_rank // rows_grid
    contract = (((0,), (0,)), ((), ()))
    direct = lax.dot_general(
        regrouped[0, :, :, :span_a], regrouped[1, :, :, span_a:], contract, preferred_element_type=jnp.float32
    )
    swapped = lax.dot_general(
        regrouped[1, :, :, :span_a], regrouped[0, :, :, span_a:], contract, preferred_element_type=jnp.float32
    )
    swapped = swapped.transpose(2, 1, 0, 3)
    virt_rows = lax.dynamic_slice_in_dim(eps_virt, row_id * span_a, span_a)
    virt_cols = lax.dynamic_slice_in_dim(eps_virt, col_id * span_b, span_b)
    occ_left = lax.dynamic_slice_in_dim(eps_occ, chosen[0] * orb_local, orb_local)
    occ_right = lax.dynamic_slice_in_dim(eps_occ, chosen[1] * orb_local, orb_local)
    denominator = (
        virt_rows[None, :, None, None]
        + virt_cols[None, None, None, :]
        - occ_left[:, None, None, None]
        - occ_right[None, None, :, None]
    )
    partial_value = -jnp.sum(direct * (2.0 * direct - swapped) / denominator, axis=3)
    partial_value = partial_value.transpose(0, 2, 1).reshape(orb_local * orb_local, span_a)
    spread = lax.dynamic_update_slice_in_dim(
        jnp.zeros((orb_local * orb_local, virt_width), jnp.float32), partial_value, row_id * span_a, 1
    )
    shares = lax.psum_scatter(spread, "aux", scatter_dimension=1, tiled=True)
    return shares.reshape(1, orb_local * orb_local, -1)


def solution(mesh):
    def on_device(factors, pair_list, eps_occ, eps_virt):
        planes = pair_list.shape[0]
        fits = (
            mesh.shape["aux"] == 2 * planes
            and mesh.shape["occ"] == 4
            and planes == 4
            and factors.shape[1] == 2
            and factors.shape[0] % 16 == 0
            and factors.shape[2] % 512 == 0
        )
        body = by_planes if fits else by_groups
        return body(factors, pair_list, eps_occ, eps_virt)

    return jax.shard_map(
        on_device,
        mesh=mesh,
        in_specs=(P("aux", "occ", None), P(), P(), P()),
        out_specs=P("occ", None, "aux"),
        check_vma=False,
    )
```

```python
import functools

import jax
import jax.numpy as jnp
from jax import lax
from jax.experimental import pallas as pl
from jax.experimental.pallas import tpu as pltpu
from jax.sharding import PartitionSpec as P

MESH = pl.DeviceIdType.MESH


def flip(z, k):
    return (z // 2 + k // 2) % 2 * 2 + (z + k) % 2


def route(
    planes, slices, pairs, e_occ, e_virt, mine, every, gath, zbuf, quarter, sel, acc, rec, held, turned, part,
    fin_send, fin_recv, o_send, o_recv, z_send, z_recv, hop_send, hop_recv, core_send, core_recv, held_sem,
):
    depth, virt = mine.shape[1], mine.shape[2]
    rows = depth // slices
    width = virt // 4
    half = virt // 2
    lag = 3
    ready = 3 * lag + 7
    steps = 2 * planes * slices
    aux = lax.axis_index("aux")
    occ = lax.axis_index("occ")
    z, x, y, c = aux // 2, aux % 2, occ // 2, occ % 2

    def device(z_, x_, y_, c_):
        return {"aux": z_ * 2 + x_, "occ": y_ * 2 + c_}

    def fellow(d):
        return {"aux": aux, "occ": flip(occ, d)}

    def source(m):
        return device(occ, m // 4, m // 2 % 2, m % 2)

    def is_me(m):
        return (occ == z) & (m == x * 4 + y * 2 + c)

    partners = [device(flip(z, k), x, y, c) for k in range(1, planes)]
    partners += [fellow(d) for d in range(1, 4)] + [device(z, 1 - x, y, c)]
    barrier = pltpu.get_barrier_semaphore()
    for partner in partners:
        pl.semaphore_signal(barrier, inc=1, device_id=partner, device_id_type=MESH)
    for m in range(8):

        @pl.when(jnp.logical_not(is_me(m)))
        def _():
            pl.semaphore_signal(barrier, inc=1, device_id=source(m), device_id_type=MESH)

    pl.semaphore_wait(barrier, len(partners) + 8 - jnp.where(z == occ, 1, 0))

    def span(t):
        return pl.ds(pl.multiple_of(t * rows, 16), rows)

    def place(s, zs, xs, ys, cs, t):
        left = pl.multiple_of((cs * 2 + ys) * width, 128)
        return gath.at[s, zs, xs, span(t), pl.ds(left, width)]

    def o_copy(t, d):
        to = flip(occ, d)
        left = pl.multiple_of((to % 2 * 2 + to // 2) * width, 128)
        src = mine.at[:, pl.ds(t * rows, rows), pl.ds(left, width)]
        if d == 0:
            return pltpu.make_async_copy(src, quarter[t].at[occ], o_recv.at[t, 0])
        return pltpu.make_async_remote_copy(
            src_ref=src,
            dst_ref=quarter[t].at[occ],
            send_sem=o_send.at[t, d],
            recv_sem=o_recv.at[t, d],
            device_id=fellow(d),
            device_id_type=MESH,
        )

    def z_copy(t, k, s, rel):
        zt = flip(z, k)
        own = x * (1 - s) + y * s
        w = own if rel == 0 else 1 - own
        dst = place(s, z, x, y, c, t) if rel == 0 else zbuf.at[k, s, span(t), :]
        return pltpu.make_async_remote_copy(
            src_ref=sel.at[t, zt, s, w],
            dst_ref=dst,
            send_sem=z_send.at[t, k, s, rel],
            recv_sem=z_recv.at[t, k, s, rel],
            device_id=device(zt, x, y, c),
            device_id_type=MESH,
        )

    def z_keep(t, s, rel):
        own = x * (1 - s) + y * s
        w = own if rel == 0 else 1 - own
        dst = place(s, z, x, y, c, t) if rel == 0 else zbuf.at[0, s, span(t), :]
        return pltpu.make_async_copy(sel.at[t, z, s, w], dst, z_recv.at[t, 0, s, rel])

    def parts_of(n):
        j = n % planes
        return n // (2 * planes), n // planes % 2, jnp.minimum(j, 1) * (1 + j % 3)

    def hop(n, kind):
        t, s, k = parts_of(n)
        zs = flip(z, k)
        xf, yf = x + s * (1 - 2 * x), y + (1 - s) * (1 - 2 * y)
        xo, yo = x + (1 - s) * (1 - 2 * x), y + s * (1 - 2 * y)
        share, other = device(z, xf, yf, c), device(z, xo, yo, c)
        own = place(s, zs, x, y, c, t)
        if kind == 0:
            src, dst, target = own, own, share
        elif kind == 1:
            src, dst, target = zbuf.at[k, s, span(t), :], own, other
        else:
            src = place(s, zs, xo, yo, c, t)
            dst, target = src, share
        return pltpu.make_async_remote_copy(
            src_ref=src,
            dst_ref=dst,
            send_sem=hop_send.at[n, kind],
            recv_sem=hop_recv.at[n, kind],
            device_id=target,
            device_id_type=MESH,
        )

    def across(n):
        t, s, k = parts_of(n)
        ref = gath.at[s, flip(z, k), :, span(t), pl.ds(pl.multiple_of(c * half, 128), half)]
        return pltpu.make_async_remote_copy(
            src_ref=ref,
            dst_ref=ref,
            send_sem=core_send.at[n],
            recv_sem=core_recv.at[n],
            device_id=device(z, x, y, 1 - c),
            device_id_type=MESH,
        )

    def fetch(t, s):
        return pltpu.make_async_copy(gath.at[s, :, :, span(t), :], held.at[t % 2, s], held_sem.at[t % 2, s])

    def start_exchange(t):
        for d in (2, 3, 1, 0):
            o_copy(t, d).start()

    def choose(t):
        for d in (0, 1, 2, 3):
            if d == 0:
                o_copy(t, d).wait()
            else:
                o_copy(t, d).wait_recv()
        for p in range(planes):
            for s in range(2):
                block = pairs[p, s]
                for w in range(2):
                    sel[t, p, s, w] = quarter[t][block, w]
        for s in range(2):
            for rel in (1, 0):
                z_keep(t, s, rel).start()
            for k in (2, 3, 1):
                for rel in (1, 0):
                    z_copy(t, k, s, rel).start()

    def last(a):
        return pltpu.make_async_remote_copy(
            src_ref=part,
            dst_ref=every.at[x * 4 + y * 2 + c],
            send_sem=fin_send.at[a],
            recv_sem=fin_recv.at[x * 4 + y * 2 + c],
            device_id={"aux": a, "occ": z},
            device_id_type=MESH,
        )

    def last_keep():
        m = x * 4 + y * 2 + c
        return pltpu.make_async_copy(part, every.at[m], fin_recv.at[m])

    def last_from(m):
        return pltpu.make_async_remote_copy(
            src_ref=part,
            dst_ref=every.at[m],
            send_sem=fin_send.at[m],
            recv_sem=fin_recv.at[m],
            device_id=source(m),
            device_id_type=MESH,
        )

    for t in range(min(2, slices)):
        start_exchange(t)

    e_i = e_occ[pairs[z, 0] * 2 + x]
    e_j = e_occ[pairs[z, 1] * 2 + y]

    choose(0)
    for t in range(2, min(4, slices)):
        start_exchange(t)

    @pl.loop(0, 2 * (half // 128))
    def _(r):
        tile, blk = r // (half // 128), r % (half // 128)
        acc[tile, pl.ds(pl.multiple_of(blk * 128, 128), 128), :] = jnp.zeros((128, half), jnp.float32)

    @pl.loop(0, 2 * (half // 128))
    def _(r):
        tile, blk = r // (half // 128), r % (half // 128)
        at = pl.ds(pl.multiple_of(blk * 128, 128), 128)
        first = pl.multiple_of((tile + c) % 2 * half + blk * 128, 128)
        far = jnp.broadcast_to(e_virt[:, pl.ds(first, 128)], (128, 128)).T
        for g in range(half // 128):
            near = e_virt[:, pl.ds(pl.multiple_of(tile * half + g * 128, 128), 128)]
            rec[tile, at, g * 128 : (g + 1) * 128] = 1.0 / (near + far - e_i - e_j)

    if slices > 1:
        choose(1)
    for t in range(4, min(6, slices)):
        start_exchange(t)

    @pl.loop(0, steps + ready + 1)
    def _(n):
        for t in range(2, slices):

            @pl.when(n == 2 * planes * (t - 2))
            def _():
                choose(t)
                if t + 4 < slices:
                    start_exchange(t + 4)

        @pl.when(n < steps)
        def _():
            t, s, k = parts_of(n)
            for rel in (1, 0):

                @pl.when(k == 0)
                def _():
                    z_keep(t, s, rel).wait()

                @pl.when(k > 0)
                def _():
                    z_copy(t, k, s, rel).wait_recv()

                hop(n, rel).start()

        @pl.when((n >= lag) & (n < steps + lag))
        def _():
            hop(n - lag, 1).wait_recv()
            hop(n - lag, 2).start()

        @pl.when((n >= 2 * lag) & (n < steps + 2 * lag))
        def _():
            hop(n - 2 * lag, 0).wait_recv()
            hop(n - 2 * lag, 2).wait_recv()
            across(n - 2 * lag).start()

        @pl.when((n >= 3 * lag) & (n < steps + 3 * lag))
        def _():
            across(n - 3 * lag).wait_recv()

        @pl.when((n >= ready) & (n < steps + ready) & ((n - ready) % 8 == 0))
        def _():
            for s in range(2):
                fetch((n - ready) // 8, s).start()

        @pl.when((n >= ready + 2) & ((n - ready) % 2 == 0))
        def _():
            t, unit = (n - ready - 2) // 8, (n - ready - 2) % 8 // 2

            @pl.when(unit == 0)
            def _():
                for s in range(2):
                    fetch(t, s).wait()

            tile = unit // 2
            top = pl.multiple_of(unit % 2 * width, 128)
            left = pl.multiple_of((tile + c) % 2 * half, 128)
            lhs = pl.multiple_of(tile * half + unit % 2 * width, 128)
            turned[...] = held[t % 2, 0, :, :, :, pl.ds(lhs, width)].reshape(2 * planes * rows, width).T

            @pl.loop(0, half // 256)
            def _(col):
                cols = pl.ds(pl.multiple_of(left + col * 256, 128), 256)
                into = pl.ds(pl.multiple_of(col * 256, 128), 256)
                acc[tile, pl.ds(top, width), into] += jnp.dot(
                    turned[...],
                    held[t % 2, 1, :, :, :, cols].reshape(2 * planes * rows, 256),
                    preferred_element_type=jnp.float32,
                )

    @pl.loop(0, 2 * (half // 128))
    def _(r):
        tile, blk = r // (half // 128), r % (half // 128)
        at = pl.ds(pl.multiple_of(blk * 128, 128), 128)
        direct = acc[tile, at, :].T
        swapped = acc[(tile + c) % 2, :, at]
        value = direct * (2.0 * direct - swapped) * rec[tile, :, at]
        part[tile, :, at] = -jnp.sum(value, axis=0, keepdims=True)

    def to_me(a):
        return (z == occ) & (a == aux)

    for a in range(8):

        @pl.when(to_me(a))
        def _():
            last_keep().start()

        @pl.when(jnp.logical_not(to_me(a)))
        def _():
            last(a).start()

    for t in range(slices):
        for d in (1, 2, 3):
            o_copy(t, d).wait_send()

    @pl.loop(0, slices)
    def _(t):
        for s in range(2):
            for rel in (1, 0):
                for k in (2, 3, 1):
                    z_copy(t, k, s, rel).wait_send()

    @pl.loop(0, steps)
    def _(n):
        for kind in range(3):
            hop(n, kind).wait_send()
        across(n).wait_send()

    for m in range(8):

        @pl.when(is_me(m))
        def _():
            last_keep().wait()

        @pl.when(jnp.logical_not(is_me(m)))
        def _():
            last_from(m).wait_recv()

    for a in range(8):

        @pl.when(jnp.logical_not(to_me(a)))
        def _():
            last(a).wait_send()


def by_planes(factors, pair_list, eps_occ, eps_virt):
    local_q, orb_local, virt = factors.shape
    n_aux = lax.axis_size("aux")
    planes = pair_list.shape[0]
    width = virt // 4
    half = virt // 2
    slices = next(n for n in (5, 3, 2, 1) if local_q % (16 * n) == 0)
    rows = local_q // slices
    steps = 2 * planes * slices
    aux = lax.axis_index("aux")
    mine = factors.transpose(1, 0, 2)

    every, _, _ = pl.pallas_call(
        functools.partial(route, planes, slices),
        out_shape=[
            jax.ShapeDtypeStruct((8, 2, 1, half), jnp.float32),
            jax.ShapeDtypeStruct((2, planes, 2, local_q, virt), factors.dtype),
            jax.ShapeDtypeStruct((planes, 2, local_q, width), factors.dtype),
        ],
        in_specs=[
            pl.BlockSpec(memory_space=pltpu.SMEM),
            pl.BlockSpec(memory_space=pltpu.SMEM),
            pl.BlockSpec(memory_space=pltpu.VMEM),
            pl.BlockSpec(memory_space=pl.ANY),
        ],
        out_specs=[
            pl.BlockSpec(memory_space=pltpu.VMEM),
            pl.BlockSpec(memory_space=pl.ANY),
            pl.BlockSpec(memory_space=pl.ANY),
        ],
        scratch_shapes=[
            [pltpu.VMEM((4, 2, rows, width), factors.dtype) for _ in range(slices)],
            pltpu.VMEM((slices, planes, 2, 2, rows, width), factors.dtype),
            pltpu.VMEM((2, half, half), jnp.float32),
            pltpu.VMEM((2, half, half), jnp.float32),
            pltpu.VMEM((2, 2, planes, 2, rows, virt), factors.dtype),
            pltpu.VMEM((width, n_aux * rows), factors.dtype),
            pltpu.VMEM((2, 1, half), jnp.float32),
            pltpu.SemaphoreType.DMA((8,)),
            pltpu.SemaphoreType.DMA((8,)),
            pltpu.SemaphoreType.DMA((slices, 4)),
            pltpu.SemaphoreType.DMA((slices, 4)),
            pltpu.SemaphoreType.DMA((slices, planes, 2, 2)),
            pltpu.SemaphoreType.DMA((slices, planes, 2, 2)),
            pltpu.SemaphoreType.DMA((steps, 3)),
            pltpu.SemaphoreType.DMA((steps, 3)),
            pltpu.SemaphoreType.DMA((steps,)),
            pltpu.SemaphoreType.DMA((steps,)),
            pltpu.SemaphoreType.DMA((2, 2)),
        ],
        compiler_params=pltpu.CompilerParams(
            collective_id=0, has_side_effects=True, vmem_limit_bytes=60 * 1024 * 1024
        ),
    )(pair_list, eps_occ, eps_virt.reshape(1, virt), mine)

    totals = every.reshape(4, 2, virt).sum(axis=1)
    return lax.dynamic_slice_in_dim(totals, aux * (virt // n_aux), virt // n_aux, 1)[None]


def by_groups(factors, pair_list, eps_occ, eps_virt):
    local_q, orb_local, virt_width = factors.shape
    aux_count = lax.axis_size("aux")
    my_group = lax.axis_index("occ")
    chosen = pair_list[my_group]
    everyone = lax.all_gather(factors, "occ", axis=1, tiled=True)
    first_block = lax.dynamic_slice_in_dim(everyone, chosen[0] * orb_local, orb_local, 1)
    second = lax.dynamic_slice_in_dim(everyone, chosen[1] * orb_local, orb_local, 1)
    picked = jnp.stack([first_block, second], axis=0)
    rows_grid = 2 ** ((aux_count.bit_length() - 1) // 2)
    cols_grid = aux_count // rows_grid
    span_a = virt_width // rows_grid
    span_b = virt_width // cols_grid
    rows_pieces = picked.reshape(2, local_q, orb_local, rows_grid, span_a).transpose(3, 0, 1, 2, 4)
    rows_pieces = jnp.tile(rows_pieces, (cols_grid, 1, 1, 1, 1))
    cols_pieces = picked.reshape(2, local_q, orb_local, cols_grid, span_b).transpose(3, 0, 1, 2, 4)
    cols_pieces = jnp.repeat(cols_pieces, rows_grid, axis=0)
    send_pieces = jnp.concatenate([rows_pieces, cols_pieces], axis=4)
    regrouped = lax.all_to_all(send_pieces, "aux", split_axis=0, concat_axis=2, tiled=True)[0]
    aux_rank = lax.axis_index("aux")
    row_id = aux_rank % rows_grid
    col_id = aux_rank // rows_grid
    contract = (((0,), (0,)), ((), ()))
    direct = lax.dot_general(
        regrouped[0, :, :, :span_a], regrouped[1, :, :, span_a:], contract, preferred_element_type=jnp.float32
    )
    swapped = lax.dot_general(
        regrouped[1, :, :, :span_a], regrouped[0, :, :, span_a:], contract, preferred_element_type=jnp.float32
    )
    swapped = swapped.transpose(2, 1, 0, 3)
    virt_rows = lax.dynamic_slice_in_dim(eps_virt, row_id * span_a, span_a)
    virt_cols = lax.dynamic_slice_in_dim(eps_virt, col_id * span_b, span_b)
    occ_left = lax.dynamic_slice_in_dim(eps_occ, chosen[0] * orb_local, orb_local)
    occ_right = lax.dynamic_slice_in_dim(eps_occ, chosen[1] * orb_local, orb_local)
    denominator = (
        virt_rows[None, :, None, None]
        + virt_cols[None, None, None, :]
        - occ_left[:, None, None, None]
        - occ_right[None, None, :, None]
    )
    partial_value = -jnp.sum(direct * (2.0 * direct - swapped) / denominator, axis=3)
    partial_value = partial_value.transpose(0, 2, 1).reshape(orb_local * orb_local, span_a)
    spread = lax.dynamic_update_slice_in_dim(
        jnp.zeros((orb_local * orb_local, virt_width), jnp.float32), partial_value, row_id * span_a, 1
    )
    shares = lax.psum_scatter(spread, "aux", scatter_dimension=1, tiled=True)
    return shares.reshape(1, orb_local * orb_local, -1)


def solution(mesh):
    def on_device(factors, pair_list, eps_occ, eps_virt):
        planes = pair_list.shape[0]
        fits = (
            mesh.shape["aux"] == 2 * planes
            and mesh.shape["occ"] == 4
            and planes == 4
            and factors.shape[1] == 2
            and factors.shape[0] % 16 == 0
            and factors.shape[2] % 512 == 0
        )
        body = by_planes if fits else by_groups
        return body(factors, pair_list, eps_occ, eps_virt)

    return jax.shard_map(
        on_device,
        mesh=mesh,
        in_specs=(P("aux", "occ", None), P(), P(), P()),
        out_specs=P("occ", None, "aux"),
        check_vma=False,
    )
```

```python
import functools

import jax
import jax.numpy as jnp
from jax import lax
from jax.experimental import pallas as pl
from jax.experimental.pallas import tpu as pltpu
from jax.sharding import PartitionSpec as P

MESH = pl.DeviceIdType.MESH


def flip(z, k):
    return (z // 2 + k // 2) % 2 * 2 + (z + k) % 2


def route(
    planes, slices, pairs, e_occ, e_virt, mine, every, gath, zbuf, quarter, sel, acc, rec, held, turned, part,
    fin_send, fin_recv, o_send, o_recv, z_send, z_recv, hop_send, hop_recv, core_send, core_recv, held_sem,
):
    depth, virt = mine.shape[1], mine.shape[2]
    rows = depth // slices
    width = virt // 4
    half = virt // 2
    lag = 3
    ready = 3 * lag + 7
    steps = 2 * planes * slices
    aux = lax.axis_index("aux")
    occ = lax.axis_index("occ")
    z, x, y, c = aux // 2, aux % 2, occ // 2, occ % 2

    inner = (z + 1) // 2 % 2

    def device(z_, x_, y_, c_):
        return {"aux": z_ * 2 + x_, "occ": y_ * 2 + c_}

    def fellow(d):
        return {"aux": aux, "occ": flip(occ, d)}

    def source(m):
        return device(occ, m // 4, m // 2 % 2, m % 2)

    def is_me(m):
        return (occ == z) & (m == x * 4 + y * 2 + c)

    partners = [device(flip(z, k), x, y, c) for k in range(1, planes)]
    partners += [fellow(d) for d in range(1, 4)] + [device(z, 1 - x, y, c)]
    barrier = pltpu.get_barrier_semaphore()
    for partner in partners:
        pl.semaphore_signal(barrier, inc=1, device_id=partner, device_id_type=MESH)
    for m in range(8):

        @pl.when(jnp.logical_not(is_me(m)))
        def _():
            pl.semaphore_signal(barrier, inc=1, device_id=source(m), device_id_type=MESH)

    pl.semaphore_wait(barrier, len(partners) + 8 - jnp.where(z == occ, 1, 0))

    def span(t):
        return pl.ds(pl.multiple_of(t * rows, 16), rows)

    def place(s, zs, xs, ys, cs, t):
        left = pl.multiple_of((cs * 2 + ys) * width, 128)
        return gath.at[s, zs, xs, span(t), pl.ds(left, width)]

    def o_copy(t, d):
        to = flip(occ, d)
        left = pl.multiple_of((to % 2 * 2 + to // 2) * width, 128)
        src = mine.at[:, pl.ds(t * rows, rows), pl.ds(left, width)]
        if d == 0:
            return pltpu.make_async_copy(src, quarter[t].at[occ], o_recv.at[t, 0])
        return pltpu.make_async_remote_copy(
            src_ref=src,
            dst_ref=quarter[t].at[occ],
            send_sem=o_send.at[t, d],
            recv_sem=o_recv.at[t, d],
            device_id=fellow(d),
            device_id_type=MESH,
        )

    def z_copy(t, k, s, rel):
        zt = flip(z, k)
        own = x * (1 - s) + y * s
        w = own if rel == 0 else 1 - own
        dst = place(s, z, x, y, c, t) if rel == 0 else zbuf.at[k, s, span(t), :]
        return pltpu.make_async_remote_copy(
            src_ref=sel.at[t, zt, s, w],
            dst_ref=dst,
            send_sem=z_send.at[t, k, s, rel],
            recv_sem=z_recv.at[t, k, s, rel],
            device_id=device(zt, x, y, c),
            device_id_type=MESH,
        )

    def z_keep(t, s, rel):
        own = x * (1 - s) + y * s
        w = own if rel == 0 else 1 - own
        dst = place(s, z, x, y, c, t) if rel == 0 else zbuf.at[0, s, span(t), :]
        return pltpu.make_async_copy(sel.at[t, z, s, w], dst, z_recv.at[t, 0, s, rel])

    def parts_of(n):
        j = n % planes
        k = j + inner * (j % 2 * (1 - j // 2) - (1 - j % 2) * (j // 2))
        return n // (2 * planes), n // planes % 2, k

    def hop(n, kind):
        t, s, k = parts_of(n)
        zs = flip(z, k)
        xf, yf = x + s * (1 - 2 * x), y + (1 - s) * (1 - 2 * y)
        xo, yo = x + (1 - s) * (1 - 2 * x), y + s * (1 - 2 * y)
        share, other = device(z, xf, yf, c), device(z, xo, yo, c)
        own = place(s, zs, x, y, c, t)
        if kind == 0:
            src, dst, target = own, own, share
        elif kind == 1:
            src, dst, target = zbuf.at[k, s, span(t), :], own, other
        else:
            src = place(s, zs, xo, yo, c, t)
            dst, target = src, share
        return pltpu.make_async_remote_copy(
            src_ref=src,
            dst_ref=dst,
            send_sem=hop_send.at[n, kind],
            recv_sem=hop_recv.at[n, kind],
            device_id=target,
            device_id_type=MESH,
        )

    def across(n):
        t, s, k = parts_of(n)
        ref = gath.at[s, flip(z, k), :, span(t), pl.ds(pl.multiple_of(c * half, 128), half)]
        return pltpu.make_async_remote_copy(
            src_ref=ref,
            dst_ref=ref,
            send_sem=core_send.at[n],
            recv_sem=core_recv.at[n],
            device_id=device(z, x, y, 1 - c),
            device_id_type=MESH,
        )

    def fetch(t, s):
        return pltpu.make_async_copy(gath.at[s, :, :, span(t), :], held.at[t % 2, s], held_sem.at[t % 2, s])

    def start_exchange(t):
        for d in (2, 3, 1, 0):
            o_copy(t, d).start()

    def choose(t):
        for d in (0, 1, 2, 3):
            if d == 0:
                o_copy(t, d).wait()
            else:
                o_copy(t, d).wait_recv()
        for p in range(planes):
            for s in range(2):
                block = pairs[p, s]
                for w in range(2):
                    sel[t, p, s, w] = quarter[t][block, w]
        for s in range(2):
            for rel in (1, 0):
                z_keep(t, s, rel).start()
            for k in (2 - inner, 1 + inner, 3):
                for rel in (1, 0):
                    z_copy(t, k, s, rel).start()

    def last(a):
        return pltpu.make_async_remote_copy(
            src_ref=part,
            dst_ref=every.at[x * 4 + y * 2 + c],
            send_sem=fin_send.at[a],
            recv_sem=fin_recv.at[x * 4 + y * 2 + c],
            device_id={"aux": a, "occ": z},
            device_id_type=MESH,
        )

    def last_keep():
        m = x * 4 + y * 2 + c
        return pltpu.make_async_copy(part, every.at[m], fin_recv.at[m])

    def last_from(m):
        return pltpu.make_async_remote_copy(
            src_ref=part,
            dst_ref=every.at[m],
            send_sem=fin_send.at[m],
            recv_sem=fin_recv.at[m],
            device_id=source(m),
            device_id_type=MESH,
        )

    for t in range(min(2, slices)):
        start_exchange(t)

    e_i = e_occ[pairs[z, 0] * 2 + x]
    e_j = e_occ[pairs[z, 1] * 2 + y]

    choose(0)
    for t in range(2, min(4, slices)):
        start_exchange(t)

    @pl.loop(0, 2 * (half // 128))
    def _(r):
        tile, blk = r // (half // 128), r % (half // 128)
        acc[tile, pl.ds(pl.multiple_of(blk * 128, 128), 128), :] = jnp.zeros((128, half), jnp.float32)

    @pl.loop(0, 2 * (half // 128))
    def _(r):
        tile, blk = r // (half // 128), r % (half // 128)
        at = pl.ds(pl.multiple_of(blk * 128, 128), 128)
        first = pl.multiple_of((tile + c) % 2 * half + blk * 128, 128)
        far = jnp.broadcast_to(e_virt[:, pl.ds(first, 128)], (128, 128)).T
        for g in range(half // 128):
            near = e_virt[:, pl.ds(pl.multiple_of(tile * half + g * 128, 128), 128)]
            rec[tile, at, g * 128 : (g + 1) * 128] = 1.0 / (near + far - e_i - e_j)

    if slices > 1:
        choose(1)
    for t in range(4, min(6, slices)):
        start_exchange(t)

    @pl.loop(0, steps + ready + 1)
    def _(n):
        for t in range(2, slices):

            @pl.when(n == 2 * planes * (t - 2))
            def _():
                choose(t)
                if t + 4 < slices:
                    start_exchange(t + 4)

        @pl.when(n < steps)
        def _():
            t, s, k = parts_of(n)
            for rel in (1, 0):

                @pl.when(k == 0)
                def _():
                    z_keep(t, s, rel).wait()

                @pl.when(k > 0)
                def _():
                    z_copy(t, k, s, rel).wait_recv()

                hop(n, rel).start()

        @pl.when((n >= lag) & (n < steps + lag))
        def _():
            hop(n - lag, 1).wait_recv()
            hop(n - lag, 2).start()

        @pl.when((n >= 2 * lag) & (n < steps + 2 * lag))
        def _():
            hop(n - 2 * lag, 0).wait_recv()
            hop(n - 2 * lag, 2).wait_recv()
            across(n - 2 * lag).start()

        @pl.when((n >= 3 * lag) & (n < steps + 3 * lag))
        def _():
            across(n - 3 * lag).wait_recv()

        @pl.when((n >= ready) & (n < steps + ready) & ((n - ready) % 8 == 0))
        def _():
            for s in range(2):
                fetch((n - ready) // 8, s).start()

        @pl.when((n >= ready + 2) & ((n - ready) % 2 == 0))
        def _():
            t, unit = (n - ready - 2) // 8, (n - ready - 2) % 8 // 2

            @pl.when(unit == 0)
            def _():
                for s in range(2):
                    fetch(t, s).wait()

            tile = unit // 2
            top = pl.multiple_of(unit % 2 * width, 128)
            left = pl.multiple_of((tile + c) % 2 * half, 128)
            lhs = pl.multiple_of(tile * half + unit % 2 * width, 128)
            turned[...] = held[t % 2, 0, :, :, :, pl.ds(lhs, width)].reshape(2 * planes * rows, width).T

            @pl.loop(0, half // 256)
            def _(col):
                cols = pl.ds(pl.multiple_of(left + col * 256, 128), 256)
                into = pl.ds(pl.multiple_of(col * 256, 128), 256)
                acc[tile, pl.ds(top, width), into] += jnp.dot(
                    turned[...],
                    held[t % 2, 1, :, :, :, cols].reshape(2 * planes * rows, 256),
                    preferred_element_type=jnp.float32,
                )

    @pl.loop(0, 2 * (half // 128))
    def _(r):
        tile, blk = r // (half // 128), r % (half // 128)
        at = pl.ds(pl.multiple_of(blk * 128, 128), 128)
        direct = acc[tile, at, :].T
        swapped = acc[(tile + c) % 2, :, at]
        value = direct * (2.0 * direct - swapped) * rec[tile, :, at]
        part[tile, :, at] = -jnp.sum(value, axis=0, keepdims=True)

    def to_me(a):
        return (z == occ) & (a == aux)

    for a in range(8):

        @pl.when(to_me(a))
        def _():
            last_keep().start()

        @pl.when(jnp.logical_not(to_me(a)))
        def _():
            last(a).start()

    for t in range(slices):
        for d in (1, 2, 3):
            o_copy(t, d).wait_send()

    @pl.loop(0, slices)
    def _(t):
        for s in range(2):
            for rel in (1, 0):
                for k in (2, 3, 1):
                    z_copy(t, k, s, rel).wait_send()

    @pl.loop(0, steps)
    def _(n):
        for kind in range(3):
            hop(n, kind).wait_send()
        across(n).wait_send()

    for m in range(8):

        @pl.when(is_me(m))
        def _():
            last_keep().wait()

        @pl.when(jnp.logical_not(is_me(m)))
        def _():
            last_from(m).wait_recv()

    for a in range(8):

        @pl.when(jnp.logical_not(to_me(a)))
        def _():
            last(a).wait_send()


def by_planes(factors, pair_list, eps_occ, eps_virt):
    local_q, orb_local, virt = factors.shape
    n_aux = lax.axis_size("aux")
    planes = pair_list.shape[0]
    width = virt // 4
    half = virt // 2
    slices = next(n for n in (5, 3, 2, 1) if local_q % (16 * n) == 0)
    rows = local_q // slices
    steps = 2 * planes * slices
    aux = lax.axis_index("aux")
    mine = factors.transpose(1, 0, 2)

    every, _, _ = pl.pallas_call(
        functools.partial(route, planes, slices),
        out_shape=[
            jax.ShapeDtypeStruct((8, 2, 1, half), jnp.float32),
            jax.ShapeDtypeStruct((2, planes, 2, local_q, virt), factors.dtype),
            jax.ShapeDtypeStruct((planes, 2, local_q, width), factors.dtype),
        ],
        in_specs=[
            pl.BlockSpec(memory_space=pltpu.SMEM),
            pl.BlockSpec(memory_space=pltpu.SMEM),
            pl.BlockSpec(memory_space=pltpu.VMEM),
            pl.BlockSpec(memory_space=pl.ANY),
        ],
        out_specs=[
            pl.BlockSpec(memory_space=pltpu.VMEM),
            pl.BlockSpec(memory_space=pl.ANY),
            pl.BlockSpec(memory_space=pl.ANY),
        ],
        scratch_shapes=[
            [pltpu.VMEM((4, 2, rows, width), factors.dtype) for _ in range(slices)],
            pltpu.VMEM((slices, planes, 2, 2, rows, width), factors.dtype),
            pltpu.VMEM((2, half, half), jnp.float32),
            pltpu.VMEM((2, half, half), jnp.float32),
            pltpu.VMEM((2, 2, planes, 2, rows, virt), factors.dtype),
            pltpu.VMEM((width, n_aux * rows), factors.dtype),
            pltpu.VMEM((2, 1, half), jnp.float32),
            pltpu.SemaphoreType.DMA((8,)),
            pltpu.SemaphoreType.DMA((8,)),
            pltpu.SemaphoreType.DMA((slices, 4)),
            pltpu.SemaphoreType.DMA((slices, 4)),
            pltpu.SemaphoreType.DMA((slices, planes, 2, 2)),
            pltpu.SemaphoreType.DMA((slices, planes, 2, 2)),
            pltpu.SemaphoreType.DMA((steps, 3)),
            pltpu.SemaphoreType.DMA((steps, 3)),
            pltpu.SemaphoreType.DMA((steps,)),
            pltpu.SemaphoreType.DMA((steps,)),
            pltpu.SemaphoreType.DMA((2, 2)),
        ],
        compiler_params=pltpu.CompilerParams(
            collective_id=0, has_side_effects=True, vmem_limit_bytes=60 * 1024 * 1024
        ),
    )(pair_list, eps_occ, eps_virt.reshape(1, virt), mine)

    totals = every.reshape(4, 2, virt).sum(axis=1)
    return lax.dynamic_slice_in_dim(totals, aux * (virt // n_aux), virt // n_aux, 1)[None]


def by_groups(factors, pair_list, eps_occ, eps_virt):
    local_q, orb_local, virt_width = factors.shape
    aux_count = lax.axis_size("aux")
    my_group = lax.axis_index("occ")
    chosen = pair_list[my_group]
    everyone = lax.all_gather(factors, "occ", axis=1, tiled=True)
    first_block = lax.dynamic_slice_in_dim(everyone, chosen[0] * orb_local, orb_local, 1)
    second = lax.dynamic_slice_in_dim(everyone, chosen[1] * orb_local, orb_local, 1)
    picked = jnp.stack([first_block, second], axis=0)
    rows_grid = 2 ** ((aux_count.bit_length() - 1) // 2)
    cols_grid = aux_count // rows_grid
    span_a = virt_width // rows_grid
    span_b = virt_width // cols_grid
    rows_pieces = picked.reshape(2, local_q, orb_local, rows_grid, span_a).transpose(3, 0, 1, 2, 4)
    rows_pieces = jnp.tile(rows_pieces, (cols_grid, 1, 1, 1, 1))
    cols_pieces = picked.reshape(2, local_q, orb_local, cols_grid, span_b).transpose(3, 0, 1, 2, 4)
    cols_pieces = jnp.repeat(cols_pieces, rows_grid, axis=0)
    send_pieces = jnp.concatenate([rows_pieces, cols_pieces], axis=4)
    regrouped = lax.all_to_all(send_pieces, "aux", split_axis=0, concat_axis=2, tiled=True)[0]
    aux_rank = lax.axis_index("aux")
    row_id = aux_rank % rows_grid
    col_id = aux_rank // rows_grid
    contract = (((0,), (0,)), ((), ()))
    direct = lax.dot_general(
        regrouped[0, :, :, :span_a], regrouped[1, :, :, span_a:], contract, preferred_element_type=jnp.float32
    )
    swapped = lax.dot_general(
        regrouped[1, :, :, :span_a], regrouped[0, :, :, span_a:], contract, preferred_element_type=jnp.float32
    )
    swapped = swapped.transpose(2, 1, 0, 3)
    virt_rows = lax.dynamic_slice_in_dim(eps_virt, row_id * span_a, span_a)
    virt_cols = lax.dynamic_slice_in_dim(eps_virt, col_id * span_b, span_b)
    occ_left = lax.dynamic_slice_in_dim(eps_occ, chosen[0] * orb_local, orb_local)
    occ_right = lax.dynamic_slice_in_dim(eps_occ, chosen[1] * orb_local, orb_local)
    denominator = (
        virt_rows[None, :, None, None]
        + virt_cols[None, None, None, :]
        - occ_left[:, None, None, None]
        - occ_right[None, None, :, None]
    )
    partial_value = -jnp.sum(direct * (2.0 * direct - swapped) / denominator, axis=3)
    partial_value = partial_value.transpose(0, 2, 1).reshape(orb_local * orb_local, span_a)
    spread = lax.dynamic_update_slice_in_dim(
        jnp.zeros((orb_local * orb_local, virt_width), jnp.float32), partial_value, row_id * span_a, 1
    )
    shares = lax.psum_scatter(spread, "aux", scatter_dimension=1, tiled=True)
    return shares.reshape(1, orb_local * orb_local, -1)


def solution(mesh):
    def on_device(factors, pair_list, eps_occ, eps_virt):
        planes = pair_list.shape[0]
        fits = (
            mesh.shape["aux"] == 2 * planes
            and mesh.shape["occ"] == 4
            and planes == 4
            and factors.shape[1] == 2
            and factors.shape[0] % 16 == 0
            and factors.shape[2] % 512 == 0
        )
        body = by_planes if fits else by_groups
        return body(factors, pair_list, eps_occ, eps_virt)

    return jax.shard_map(
        on_device,
        mesh=mesh,
        in_specs=(P("aux", "occ", None), P(), P(), P()),
        out_specs=P("occ", None, "aux"),
        check_vma=False,
    )
```

```python
import functools

import jax
import jax.numpy as jnp
from jax import lax
from jax.experimental import pallas as pl
from jax.experimental.pallas import tpu as pltpu
from jax.sharding import PartitionSpec as P

MESH = pl.DeviceIdType.MESH


def flip(z, k):
    return (z // 2 + k // 2) % 2 * 2 + (z + k) % 2


def route(
    planes, slices, pairs, e_occ, e_virt, mine, every, gath, zbuf, quarter, sel, acc, rec, held, turned, part,
    fin_send, fin_recv, o_send, o_recv, z_send, z_recv, hop_send, hop_recv, core_send, core_recv, held_sem,
):
    depth, virt = mine.shape[1], mine.shape[2]
    rows = depth // slices
    width = virt // 4
    half = virt // 2
    lag = 2
    ready = 3 * lag + 7
    steps = 2 * planes * slices
    aux = lax.axis_index("aux")
    occ = lax.axis_index("occ")
    z, x, y, c = aux // 2, aux % 2, occ // 2, occ % 2

    inner = (z + 1) // 2 % 2

    def device(z_, x_, y_, c_):
        return {"aux": z_ * 2 + x_, "occ": y_ * 2 + c_}

    def fellow(d):
        return {"aux": aux, "occ": flip(occ, d)}

    def source(m):
        return device(occ, m // 4, m // 2 % 2, m % 2)

    def is_me(m):
        return (occ == z) & (m == x * 4 + y * 2 + c)

    partners = [device(flip(z, k), x, y, c) for k in range(1, planes)]
    partners += [fellow(d) for d in range(1, 4)] + [device(z, 1 - x, y, c)]
    barrier = pltpu.get_barrier_semaphore()
    for partner in partners:
        pl.semaphore_signal(barrier, inc=1, device_id=partner, device_id_type=MESH)
    for m in range(8):

        @pl.when(jnp.logical_not(is_me(m)))
        def _():
            pl.semaphore_signal(barrier, inc=1, device_id=source(m), device_id_type=MESH)

    pl.semaphore_wait(barrier, len(partners) + 8 - jnp.where(z == occ, 1, 0))

    def span(t):
        return pl.ds(pl.multiple_of(t * rows, 16), rows)

    def place(s, zs, xs, ys, cs, t):
        left = pl.multiple_of((cs * 2 + ys) * width, 128)
        return gath.at[s, zs, xs, span(t), pl.ds(left, width)]

    def o_copy(t, d):
        to = flip(occ, d)
        left = pl.multiple_of((to % 2 * 2 + to // 2) * width, 128)
        src = mine.at[:, pl.ds(t * rows, rows), pl.ds(left, width)]
        if d == 0:
            return pltpu.make_async_copy(src, quarter[t].at[occ], o_recv.at[t, 0])
        return pltpu.make_async_remote_copy(
            src_ref=src,
            dst_ref=quarter[t].at[occ],
            send_sem=o_send.at[t, d],
            recv_sem=o_recv.at[t, d],
            device_id=fellow(d),
            device_id_type=MESH,
        )

    def z_copy(t, k, s, rel):
        zt = flip(z, k)
        own = x * (1 - s) + y * s
        w = own if rel == 0 else 1 - own
        dst = place(s, z, x, y, c, t) if rel == 0 else zbuf.at[k, s, span(t), :]
        return pltpu.make_async_remote_copy(
            src_ref=sel.at[t, zt, s, w],
            dst_ref=dst,
            send_sem=z_send.at[t, k, s, rel],
            recv_sem=z_recv.at[t, k, s, rel],
            device_id=device(zt, x, y, c),
            device_id_type=MESH,
        )

    def z_keep(t, s, rel):
        own = x * (1 - s) + y * s
        w = own if rel == 0 else 1 - own
        dst = place(s, z, x, y, c, t) if rel == 0 else zbuf.at[0, s, span(t), :]
        return pltpu.make_async_copy(sel.at[t, z, s, w], dst, z_recv.at[t, 0, s, rel])

    def parts_of(n):
        j = n % planes
        k = j + inner * (j % 2 * (1 - j // 2) - (1 - j % 2) * (j // 2))
        return n // (2 * planes), n // planes % 2, k

    def hop(n, kind):
        t, s, k = parts_of(n)
        zs = flip(z, k)
        xf, yf = x + s * (1 - 2 * x), y + (1 - s) * (1 - 2 * y)
        xo, yo = x + (1 - s) * (1 - 2 * x), y + s * (1 - 2 * y)
        share, other = device(z, xf, yf, c), device(z, xo, yo, c)
        own = place(s, zs, x, y, c, t)
        if kind == 0:
            src, dst, target = own, own, share
        elif kind == 1:
            src, dst, target = zbuf.at[k, s, span(t), :], own, other
        else:
            src = place(s, zs, xo, yo, c, t)
            dst, target = src, share
        return pltpu.make_async_remote_copy(
            src_ref=src,
            dst_ref=dst,
            send_sem=hop_send.at[n, kind],
            recv_sem=hop_recv.at[n, kind],
            device_id=target,
            device_id_type=MESH,
        )

    def across(n):
        t, s, k = parts_of(n)
        ref = gath.at[s, flip(z, k), :, span(t), pl.ds(pl.multiple_of(c * half, 128), half)]
        return pltpu.make_async_remote_copy(
            src_ref=ref,
            dst_ref=ref,
            send_sem=core_send.at[n],
            recv_sem=core_recv.at[n],
            device_id=device(z, x, y, 1 - c),
            device_id_type=MESH,
        )

    def fetch(t, s):
        return pltpu.make_async_copy(gath.at[s, :, :, span(t), :], held.at[s], held_sem.at[s])

    def start_exchange(t):
        for d in (2, 3, 1, 0):
            o_copy(t, d).start()

    def choose(t):
        for d in (0, 1, 2, 3):
            if d == 0:
                o_copy(t, d).wait()
            else:
                o_copy(t, d).wait_recv()
        for p in range(planes):
            for s in range(2):
                block = pairs[p, s]
                for w in range(2):
                    sel[t, p, s, w] = quarter[t][block, w]
        for s in range(2):
            for rel in (1, 0):
                z_keep(t, s, rel).start()
            for k in (2 - inner, 1 + inner, 3):
                for rel in (1, 0):
                    z_copy(t, k, s, rel).start()

    def last(a):
        return pltpu.make_async_remote_copy(
            src_ref=part,
            dst_ref=every.at[x * 4 + y * 2 + c],
            send_sem=fin_send.at[a],
            recv_sem=fin_recv.at[x * 4 + y * 2 + c],
            device_id={"aux": a, "occ": z},
            device_id_type=MESH,
        )

    def last_keep():
        m = x * 4 + y * 2 + c
        return pltpu.make_async_copy(part, every.at[m], fin_recv.at[m])

    def last_from(m):
        return pltpu.make_async_remote_copy(
            src_ref=part,
            dst_ref=every.at[m],
            send_sem=fin_send.at[m],
            recv_sem=fin_recv.at[m],
            device_id=source(m),
            device_id_type=MESH,
        )

    start_exchange(0)

    e_i = e_occ[pairs[z, 0] * 2 + x]
    e_j = e_occ[pairs[z, 1] * 2 + y]

    choose(0)
    for t in range(1, min(3, slices)):
        start_exchange(t)

    @pl.loop(0, 2 * (half // 128))
    def _(r):
        tile, blk = r // (half // 128), r % (half // 128)
        acc[tile, pl.ds(pl.multiple_of(blk * 128, 128), 128), :] = jnp.zeros((128, half), jnp.float32)

    @pl.loop(0, 2 * (half // 128))
    def _(r):
        tile, blk = r // (half // 128), r % (half // 128)
        at = pl.ds(pl.multiple_of(blk * 128, 128), 128)
        first = pl.multiple_of((tile + c) % 2 * half + blk * 128, 128)
        far = jnp.broadcast_to(e_virt[:, pl.ds(first, 128)], (128, 128)).T
        for g in range(half // 128):
            near = e_virt[:, pl.ds(pl.multiple_of(tile * half + g * 128, 128), 128)]
            rec[tile, at, g * 128 : (g + 1) * 128] = 1.0 / (near + far - e_i - e_j)

    @pl.loop(0, steps + ready - 3)
    def _(n):
        for t in range(1, slices):

            @pl.when(n == 2 * planes * (t - 1) + 1)
            def _():
                choose(t)
                if t + 2 < slices:
                    start_exchange(t + 2)

        @pl.when(n < steps)
        def _():
            t, s, k = parts_of(n)
            for rel in (1, 0):

                @pl.when(k == 0)
                def _():
                    z_keep(t, s, rel).wait()

                @pl.when(k > 0)
                def _():
                    z_copy(t, k, s, rel).wait_recv()

                hop(n, rel).start()

        @pl.when((n >= lag) & (n < steps + lag))
        def _():
            hop(n - lag, 1).wait_recv()
            hop(n - lag, 2).start()

        @pl.when((n >= 2 * lag) & (n < steps + 2 * lag))
        def _():
            hop(n - 2 * lag, 0).wait_recv()
            hop(n - 2 * lag, 2).wait_recv()
            across(n - 2 * lag).start()

        @pl.when((n >= 3 * lag) & (n < steps + 3 * lag))
        def _():
            across(n - 3 * lag).wait_recv()

        @pl.when((n >= ready) & (n < steps + ready) & ((n - ready) % 8 == 0))
        def _():
            for s in range(2):
                fetch((n - ready) // 8, s).start()

        @pl.when((n >= ready + 1) & ((n - ready - 1) % 8 < 4))
        def _():
            t, unit = (n - ready - 1) // 8, (n - ready - 1) % 8

            @pl.when(unit == 0)
            def _():
                for s in range(2):
                    fetch(t, s).wait()

            tile = unit // 2
            top = pl.multiple_of(unit % 2 * width, 128)
            left = pl.multiple_of((tile + c) % 2 * half, 128)
            lhs = pl.multiple_of(tile * half + unit % 2 * width, 128)
            turned[...] = held[0, :, :, :, pl.ds(lhs, width)].reshape(2 * planes * rows, width).T

            @pl.loop(0, half // 256)
            def _(col):
                cols = pl.ds(pl.multiple_of(left + col * 256, 128), 256)
                into = pl.ds(pl.multiple_of(col * 256, 128), 256)
                acc[tile, pl.ds(top, width), into] += jnp.dot(
                    turned[...],
                    held[1, :, :, :, cols].reshape(2 * planes * rows, 256),
                    preferred_element_type=jnp.float32,
                )

    @pl.loop(0, 2 * (half // 128))
    def _(r):
        tile, blk = r // (half // 128), r % (half // 128)
        at = pl.ds(pl.multiple_of(blk * 128, 128), 128)
        direct = acc[tile, at, :].T
        swapped = acc[(tile + c) % 2, :, at]
        value = direct * (2.0 * direct - swapped) * rec[tile, :, at]
        part[tile, :, at] = -jnp.sum(value, axis=0, keepdims=True)

    def to_me(a):
        return (z == occ) & (a == aux)

    for a in range(8):

        @pl.when(to_me(a))
        def _():
            last_keep().start()

        @pl.when(jnp.logical_not(to_me(a)))
        def _():
            last(a).start()

    for t in range(slices):
        for d in (1, 2, 3):
            o_copy(t, d).wait_send()

    @pl.loop(0, slices)
    def _(t):
        for s in range(2):
            for rel in (1, 0):
                for k in (2, 3, 1):
                    z_copy(t, k, s, rel).wait_send()

    @pl.loop(0, steps)
    def _(n):
        for kind in range(3):
            hop(n, kind).wait_send()
        across(n).wait_send()

    for m in range(8):

        @pl.when(is_me(m))
        def _():
            last_keep().wait()

        @pl.when(jnp.logical_not(is_me(m)))
        def _():
            last_from(m).wait_recv()

    for a in range(8):

        @pl.when(jnp.logical_not(to_me(a)))
        def _():
            last(a).wait_send()


def by_planes(factors, pair_list, eps_occ, eps_virt):
    local_q, orb_local, virt = factors.shape
    n_aux = lax.axis_size("aux")
    planes = pair_list.shape[0]
    width = virt // 4
    half = virt // 2
    slices = next(n for n in (3, 2, 1) if local_q % (16 * n) == 0)
    rows = local_q // slices
    steps = 2 * planes * slices
    aux = lax.axis_index("aux")
    mine = factors.transpose(1, 0, 2)

    every, _, _ = pl.pallas_call(
        functools.partial(route, planes, slices),
        out_shape=[
            jax.ShapeDtypeStruct((8, 2, 1, half), jnp.float32),
            jax.ShapeDtypeStruct((2, planes, 2, local_q, virt), factors.dtype),
            jax.ShapeDtypeStruct((planes, 2, local_q, width), factors.dtype),
        ],
        in_specs=[
            pl.BlockSpec(memory_space=pltpu.SMEM),
            pl.BlockSpec(memory_space=pltpu.SMEM),
            pl.BlockSpec(memory_space=pltpu.VMEM),
            pl.BlockSpec(memory_space=pl.ANY),
        ],
        out_specs=[
            pl.BlockSpec(memory_space=pltpu.VMEM),
            pl.BlockSpec(memory_space=pl.ANY),
            pl.BlockSpec(memory_space=pl.ANY),
        ],
        scratch_shapes=[
            [pltpu.VMEM((4, 2, rows, width), factors.dtype) for _ in range(slices)],
            pltpu.VMEM((slices, planes, 2, 2, rows, width), factors.dtype),
            pltpu.VMEM((2, half, half), jnp.float32),
            pltpu.VMEM((2, half, half), jnp.float32),
            pltpu.VMEM((2, planes, 2, rows, virt), factors.dtype),
            pltpu.VMEM((width, n_aux * rows), factors.dtype),
            pltpu.VMEM((2, 1, half), jnp.float32),
            pltpu.SemaphoreType.DMA((8,)),
            pltpu.SemaphoreType.DMA((8,)),
            pltpu.SemaphoreType.DMA((slices, 4)),
            pltpu.SemaphoreType.DMA((slices, 4)),
            pltpu.SemaphoreType.DMA((slices, planes, 2, 2)),
            pltpu.SemaphoreType.DMA((slices, planes, 2, 2)),
            pltpu.SemaphoreType.DMA((steps, 3)),
            pltpu.SemaphoreType.DMA((steps, 3)),
            pltpu.SemaphoreType.DMA((steps,)),
            pltpu.SemaphoreType.DMA((steps,)),
            pltpu.SemaphoreType.DMA((2,)),
        ],
        compiler_params=pltpu.CompilerParams(
            collective_id=0, has_side_effects=True, vmem_limit_bytes=60 * 1024 * 1024
        ),
    )(pair_list, eps_occ, eps_virt.reshape(1, virt), mine)

    totals = every.reshape(4, 2, virt).sum(axis=1)
    return lax.dynamic_slice_in_dim(totals, aux * (virt // n_aux), virt // n_aux, 1)[None]


def by_groups(factors, pair_list, eps_occ, eps_virt):
    local_q, orb_local, virt_width = factors.shape
    aux_count = lax.axis_size("aux")
    my_group = lax.axis_index("occ")
    chosen = pair_list[my_group]
    everyone = lax.all_gather(factors, "occ", axis=1, tiled=True)
    first_block = lax.dynamic_slice_in_dim(everyone, chosen[0] * orb_local, orb_local, 1)
    second = lax.dynamic_slice_in_dim(everyone, chosen[1] * orb_local, orb_local, 1)
    picked = jnp.stack([first_block, second], axis=0)
    rows_grid = 2 ** ((aux_count.bit_length() - 1) // 2)
    cols_grid = aux_count // rows_grid
    span_a = virt_width // rows_grid
    span_b = virt_width // cols_grid
    rows_pieces = picked.reshape(2, local_q, orb_local, rows_grid, span_a).transpose(3, 0, 1, 2, 4)
    rows_pieces = jnp.tile(rows_pieces, (cols_grid, 1, 1, 1, 1))
    cols_pieces = picked.reshape(2, local_q, orb_local, cols_grid, span_b).transpose(3, 0, 1, 2, 4)
    cols_pieces = jnp.repeat(cols_pieces, rows_grid, axis=0)
    send_pieces = jnp.concatenate([rows_pieces, cols_pieces], axis=4)
    regrouped = lax.all_to_all(send_pieces, "aux", split_axis=0, concat_axis=2, tiled=True)[0]
    aux_rank = lax.axis_index("aux")
    row_id = aux_rank % rows_grid
    col_id = aux_rank // rows_grid
    contract = (((0,), (0,)), ((), ()))
    direct = lax.dot_general(
        regrouped[0, :, :, :span_a], regrouped[1, :, :, span_a:], contract, preferred_element_type=jnp.float32
    )
    swapped = lax.dot_general(
        regrouped[1, :, :, :span_a], regrouped[0, :, :, span_a:], contract, preferred_element_type=jnp.float32
    )
    swapped = swapped.transpose(2, 1, 0, 3)
    virt_rows = lax.dynamic_slice_in_dim(eps_virt, row_id * span_a, span_a)
    virt_cols = lax.dynamic_slice_in_dim(eps_virt, col_id * span_b, span_b)
    occ_left = lax.dynamic_slice_in_dim(eps_occ, chosen[0] * orb_local, orb_local)
    occ_right = lax.dynamic_slice_in_dim(eps_occ, chosen[1] * orb_local, orb_local)
    denominator = (
        virt_rows[None, :, None, None]
        + virt_cols[None, None, None, :]
        - occ_left[:, None, None, None]
        - occ_right[None, None, :, None]
    )
    partial_value = -jnp.sum(direct * (2.0 * direct - swapped) / denominator, axis=3)
    partial_value = partial_value.transpose(0, 2, 1).reshape(orb_local * orb_local, span_a)
    spread = lax.dynamic_update_slice_in_dim(
        jnp.zeros((orb_local * orb_local, virt_width), jnp.float32), partial_value, row_id * span_a, 1
    )
    shares = lax.psum_scatter(spread, "aux", scatter_dimension=1, tiled=True)
    return shares.reshape(1, orb_local * orb_local, -1)


def solution(mesh):
    def on_device(factors, pair_list, eps_occ, eps_virt):
        planes = pair_list.shape[0]
        fits = (
            mesh.shape["aux"] == 2 * planes
            and mesh.shape["occ"] == 4
            and planes == 4
            and factors.shape[1] == 2
            and factors.shape[0] % 16 == 0
            and factors.shape[2] % 512 == 0
        )
        body = by_planes if fits else by_groups
        return body(factors, pair_list, eps_occ, eps_virt)

    return jax.shard_map(
        on_device,
        mesh=mesh,
        in_specs=(P("aux", "occ", None), P(), P(), P()),
        out_specs=P("occ", None, "aux"),
        check_vma=False,
    )
```
